128 devices in a mesh: slab: 8 (over x_lo, y), rel: 16 (over z, x_hi, core).
Axes of the slice: x: 4 (x_hi: 2, x_lo: 2; x = x_hi * 2 + x_lo), y: 4, z: 4, core: 2. Of those that a mesh axis runs over, the one named last changes fastest.
Arguments:
- concentration: float32 [64, 4, 512, 1024], P('rel', None, 'slab'), may hold values from 0 to 2
- wind_store: bfloat16 [32, 4, 4, 512, 1024], P('rel', None, None, 'slab'), may hold values from -0.45 to 0.45, as said below
- sources: int32 [64], P('rel'), may hold values from 0 to 2097151
- emission: float32 [64], P('rel'), may hold values from 1 to 4
- snapshot_ids: int32 [2], replicated, may hold values from 0 to 31
Outputs:
- advanced: float32 [64, 4, 512, 1024], P('rel', None, 'slab')
The draws below stay inside these ranges and needn't reach their ends.
Inputs may be any that keep to these rules, and one draw needn't show every extreme that they name: `wind_store`: channels 0 to 2 are Courant numbers of magnitude at most 0.45, channel 3 a diffusion number between 0.01 and 0.12.
All inputs are finite; a program needn't handle non-finite values.
Results may differ from the reference program's by a relative error of at most 0.0003.
Values may be sent and summed in bfloat16 or wider, within the bound.
No kernel may reach another device: no remote copies, remote signals or barrier semaphores. Data moves between devices by JAX's collectives and lax.ppermute only.
A program may use at most 192 MiB of HBM per device.

```python
import math
import jax
import jax.numpy as jnp
from jax import lax

NY = 1024
NZ = 4
STEPS = 2
NX = 512
RELEASES = 64
SNAPS = 32


def draw_wind_store(key, part):
    key = jax.random.fold_in(key, 7)
    first_key, second_key = jax.random.split(key)
    shape = (SNAPS, 3, NZ, NX, NY)
    courant = jnp.clip(0.2 * jax.random.normal(first_key, shape, jnp.float32), -0.45, 0.45)
    logs = jax.random.uniform(second_key, (SNAPS, 1, NZ, NX, NY), jnp.float32, math.log(0.01), math.log(0.12))
    return jnp.concatenate([courant, jnp.exp(logs)], axis=1).astype(jnp.bfloat16)


def with_ends(values, rng, low, largest):
    index_at = [jax.random.randint(jax.random.fold_in(rng, axis), (), 0, length) for axis, length in enumerate(values.shape)]
    widest = values.shape.index(max(values.shape))
    neighbour = index_at[:widest] + [(index_at[widest] + 1) % values.shape[widest]] + index_at[widest + 1:]
    return values.at[tuple(index_at)].set(low).at[tuple(neighbour)].set(largest)


def levels(stream_key, dims, shards, least, largest):
    gain = 1.0
    for axis_at, shards_of in shards:
        steps = jax.random.uniform(jax.random.fold_in(jax.random.fold_in(stream_key, 6), axis_at), (shards_of,), jnp.float32, least / len(shards), largest / len(shards))
        gain = gain * jnp.repeat(jnp.exp(steps), dims[axis_at] // shards_of).reshape((-1,) + (1,) * (len(dims) - 1 - axis_at))
    return gain


def setup_inputs(seed: int = 0) -> dict:
    seeds = jax.random.split(jax.random.key(seed), 6)
    return {
        "concentration": jnp.clip(2.0 * jax.random.uniform(seeds[0], (RELEASES, NZ, NX, NY), jnp.float32) ** levels(seeds[0], (RELEASES, NZ, NX, NY), ((0, 16), (2, 8)), -0.2, 0.2), 0.0, 2.0),
        "wind_store": draw_wind_store(jax.random.fold_in(seeds[5], 71), 0),
        "sources": with_ends(jax.random.randint(seeds[2], (RELEASES,), 0, NZ * NX * NY), jax.random.fold_in(seeds[2], 1), 0, (NZ * NX * NY) - 1).astype(jnp.int32),
        "emission": jnp.clip(jnp.exp(math.log(4.0) - 1.3862944 * jax.random.uniform(seeds[3], (RELEASES,), jnp.float32) ** levels(seeds[3], (RELEASES,), ((0, 16),), -0.2, 0.2)), 1.0, 4.0),
        "snapshot_ids": jax.random.randint(seeds[4], (STEPS,), 0, SNAPS).astype(jnp.int32),
    }


def central(first, second, fourth, fifth):
    return (first - 8.0 * second + 8.0 * fourth - fifth) / 12.0


def quartic(first, second, middle, fourth, fifth):
    return (first - 4.0 * second + 6.0 * middle - 4.0 * fourth + fifth) / 12.0


def advance(field, padded, diffus_pad, courant):
    west_two = padded[..., 0:-4, :]
    west_one = padded[..., 1:-3, :]
    east_one = padded[..., 3:-1, :]
    east_two = padded[..., 4:, :]
    south_two = jnp.roll(field, 2, -1)
    south_one = jnp.roll(field, 1, -1)
    north_one = jnp.roll(field, -1, -1)
    north_two = jnp.roll(field, -2, -1)
    widths = [(0, 0)] * (field.ndim - 3) + [(2, 2), (0, 0), (0, 0)]
    levels_pad = jnp.pad(field, widths, mode="edge")
    below_two = levels_pad[..., 0:-4, :, :]
    below_one = levels_pad[..., 1:-3, :, :]
    above_one = levels_pad[..., 3:-1, :, :]
    above_two = levels_pad[..., 4:, :, :]
    advected = courant[0] * central(west_two, west_one, east_one, east_two)
    advected = advected + jnp.abs(courant[0]) * quartic(west_two, west_one, field, east_one, east_two)
    advected = advected + courant[1] * central(south_two, south_one, north_one, north_two)
    advected = advected + jnp.abs(courant[1]) * quartic(south_two, south_one, field, north_one, north_two)
    advected = advected + courant[2] * central(below_two, below_one, above_one, above_two)
    advected = advected + jnp.abs(courant[2]) * quartic(below_two, below_one, field, above_one, above_two)
    diffus = diffus_pad[:, 1:-1, :]
    face_east = 0.5 * (diffus + diffus_pad[:, 2:, :])
    face_west = 0.5 * (diffus + diffus_pad[:, :-2, :])
    face_north = 0.5 * (diffus + jnp.roll(diffus, -1, -1))
    face_south = 0.5 * (diffus + jnp.roll(diffus, 1, -1))
    diffus_levels = jnp.pad(diffus, ((1, 1), (0, 0), (0, 0)), mode="edge")
    face_above = 0.5 * (diffus + diffus_levels[2:])
    face_below = 0.5 * (diffus + diffus_levels[:-2])
    spread = face_east * (east_one - field) - face_west * (field - west_one)
    spread = spread + face_north * (north_one - field) - face_south * (field - south_one)
    spread = spread + face_above * (above_one - field) - face_below * (field - below_one)
    return field - advected + spread


def reference(concentration, wind_store, sources, emission, snapshot_ids):
    cell_ids = jnp.arange(NZ * NX * NY, dtype=jnp.int32).reshape(NZ, NX, NY)

    def one_release(inputs):
        field, source_cell, amount = inputs
        emitted = amount * (cell_ids == source_cell).astype(jnp.float32)
        for number in range(STEPS):
            snapshot = lax.dynamic_index_in_dim(wind_store, snapshot_ids[number], 0, keepdims=False).astype(jnp.float32)
            padded = jnp.pad(field, ((0, 0), (2, 2), (0, 0)))
            diffus_pad = jnp.pad(snapshot[3], ((0, 0), (1, 1), (0, 0)))
            field = advance(field, padded, diffus_pad, snapshot[0:3]) + emitted
        return field

    return lax.map(one_release, (concentration, sources, emission))
```

```python
import functools
import jax
import jax.numpy as jnp
from jax import lax
from jax.experimental import pallas as pl
from jax.experimental.pallas import tpu as pltpu
from jax.sharding import PartitionSpec as P

LANES = 128
PAD = 8


PIECES = 4
PIECE = (4, 2, 16, 1024)
LINKS = 3
PHASES = 4

SCHEDULES = (
    (
        (2, 4, 5, -1, -1, -1, -1, -1, -1, -1, -1, -1, -1, -1, -1, -1, -1, -1, -1, -1, -1, -1, -1, -1),
        (3, 7, 6, 5, 5, -1, 2, -1, 2, -1, -1, -1, -1, -1, -1, -1, -1, -1, -1, -1, 4, -1, -1, -1),
        (7, 1, 0, 6, 6, -1, 3, -1, 3, 5, -1, 5, 2, -1, 2, -1, -1, -1, 7, 4, 7, -1, 4, 5),
        (1, 0, 1, 0, 0, 0, 7, 2, 7, -1, 3, 6, 3, -1, 3, 2, -1, 5, -1, 1, -1, 4, 6, -1),
        (7, 7, 7, 4, 1, 5, 3, 6, 1, 0, 0, 0, 1, 4, 1, 3, 6, 6, 4, 0, 5, 2, 7, 6),
    ),
    (
        (0, 3, 1, 5, 7, 6, -1, -1, -1, -1, -1, -1, -1, -1, -1, -1, -1, -1, -1, -1, -1, -1, -1, -1),
        (1, 2, 2, 4, 6, 4, 0, -1, 0, 5, -1, 5, -1, -1, -1, -1, -1, -1, -1, 3, 3, -1, 7, 7),
        (6, 4, 3, 2, 1, -1, 1, -1, -1, 4, 5, 4, 3, 3, 0, 5, 7, 7, 7, 2, 2, 6, 6, 6),
        (7, 0, 1, 1, 7, 5, 5, 6, 3, 2, 0, 2, 1, 1, 1, 0, 6, 6, 4, 4, 4, 2, 3, 5),
        (-1, -1, -1, -1, -1, -1, -1, -1, -1, -1, -1, -1, -1, -1, -1, -1, -1, -1, -1, -1, -1, -1, -1, -1),
    ),
    (
        (0, 3, 0, -1, -1, -1, 6, 5, 7, -1, -1, -1, -1, -1, -1, -1, -1, -1, -1, -1, -1, -1, -1, -1),
        (1, 2, 1, -1, 0, -1, 4, 7, 5, 7, 7, -1, 6, -1, 6, -1, -1, -1, -1, 3, 3, -1, -1, -1),
        (2, 5, 2, 0, 7, 1, 1, 4, 1, 5, 5, -1, 4, 3, 4, 6, 6, 7, -1, 6, 2, 3, 0, 0),
        (7, 7, 4, 2, 1, 5, 2, 6, 3, 1, 0, 0, 1, 4, 3, 5, 4, 5, 4, 0, 4, 6, 2, -1),
        (-1, -1, -1, -1, -1, -1, -1, -1, -1, -1, -1, -1, -1, -1, -1, -1, -1, -1, -1, -1, -1, -1, -1, -1),
    ),
    (
        (0, 2, 1, -1, -1, -1, -1, -1, -1, 6, 4, 5, -1, -1, -1, -1, -1, -1, -1, -1, -1, -1, -1, -1),
        (3, 3, 0, 1, 1, 4, 0, 5, 0, 4, 5, 7, -1, -1, -1, -1, -1, 6, -1, 2, 2, -1, -1, -1),
        (1, 5, 3, -1, 0, -1, 7, 7, 3, 5, 7, 6, 6, 2, 2, 4, 4, 4, -1, -1, 3, -1, 1, 1),
        (7, 7, 1, 7, 7, 5, 1, 6, 3, 3, 6, 0, 0, 4, 7, 5, 2, 5, -1, 3, 6, 2, 0, 4),
        (-1, -1, -1, -1, -1, -1, -1, -1, -1, -1, -1, -1, -1, -1, -1, -1, -1, -1, -1, -1, -1, -1, -1, -1),
    ),
    (
        (0, 2, 3, -1, -1, -1, -1, -1, -1, -1, -1, -1, 6, 7, 5, -1, -1, -1, -1, -1, -1, -1, -1, -1),
        (1, 1, 1, 3, 3, -1, 0, 7, 0, -1, -1, -1, 4, 6, 4, -1, 5, -1, -1, 2, 6, -1, -1, -1),
        (3, 3, 7, 1, 1, 1, 1, 0, 6, 0, 5, -1, 5, 2, 2, 4, 4, -1, 2, 4, 2, 6, 3, 6),
        (7, 7, 0, 7, 7, 5, 6, 6, 3, 6, 4, 5, 0, 4, 7, 0, 2, 5, 4, 3, 5, 2, 1, 2),
        (-1, -1, -1, -1, -1, -1, -1, -1, -1, -1, -1, -1, -1, -1, -1, -1, -1, -1, -1, -1, -1, -1, -1, -1),
    ),
    (
        (1, 3, 0, -1, -1, -1, -1, -1, -1, -1, -1, -1, -1, -1, -1, 7, 5, 4, -1, -1, -1, -1, -1, -1),
        (0, 2, 1, -1, 0, -1, 1, -1, -1, -1, -1, 5, 4, -1, -1, 5, 6, 6, -1, 3, -1, 7, 7, 7),
        (2, 3, 3, 1, 1, 7, 0, 5, 0, 6, 6, 6, 6, 3, 3, 4, 4, 7, 4, 2, 2, 5, 0, 0),
        (7, 5, 4, 7, 3, 5, 6, 6, 2, 1, 0, 4, 1, 1, 7, 5, 3, 5, 4, 3, 6, 2, 2, 2),
        (-1, -1, -1, -1, -1, -1, -1, -1, -1, -1, -1, -1, -1, -1, -1, -1, -1, -1, -1, -1, -1, -1, -1, -1),
    ),
    (
        (0, 1, 1, -1, -1, -1, -1, -1, -1, -1, -1, -1, -1, -1, -1, -1, -1, -1, 6, 5, 7, -1, -1, -1),
        (2, 3, 6, 1, -1, -1, 0, -1, 0, -1, -1, -1, -1, -1, 5, -1, -1, -1, 7, 4, 4, 7, 7, -1),
        (3, 7, 2, 6, 6, -1, 2, 0, 2, 1, -1, 1, 0, 4, 0, 5, 5, 7, -1, 1, 3, 4, 4, -1),
        (6, 3, 3, 7, 2, 4, 3, -1, 3, 6, 0, 5, 2, 7, 2, 1, 4, -1, 5, 6, 0, 5, 3, 4),
        (-1, -1, -1, -1, -1, -1, -1, -1, -1, -1, -1, -1, -1, -1, -1, -1, -1, -1, -1, -1, -1, -1, -1, -1),
    ),
    (
        (3, 1, 2, -1, -1, -1, -1, -1, -1, -1, -1, -1, -1, -1, -1, -1, -1, -1, -1, -1, -1, 5, 6, 7),
        (0, 3, 0, 2, 2, 5, 3, -1, 3, -1, -1, -1, -1, -1, -1, -1, 6, 6, 7, 1, -1, 4, 4, 4),
        (2, 5, 1, 5, 0, 0, -1, 3, 0, 2, 6, 6, 1, 1, 1, -1, -1, 4, 4, 7, 3, 7, 5, 2),
        (7, 0, 3, 7, 7, 5, 0, 6, 1, 3, 0, 5, -1, 4, 7, 1, 4, 5, 4, 2, 5, 2, 0, 6),
        (-1, -1, -1, -1, -1, -1, -1, -1, -1, -1, -1, -1, -1, -1, -1, -1, -1, -1, -1, -1, -1, -1, -1, -1),
    ),
)


def piece_of(tile, piece, half):
    at = pl.multiple_of(half * 32 + 16 * (piece // 2), 16)
    return tile.at[:, pl.ds(2 * (piece % 2), 2), pl.ds(at, 16), :]


def plan(ids_ref, table_ref):
    chip = lax.axis_index("rel") >> 1
    first = ids_ref[0] >> 2
    second = ids_ref[1] >> 2

    def place(of):
        return 2 * (((of >> 1) - (first >> 1)) & 3) + ((of ^ first) & 1)

    here = place(chip)
    row = place(second) * 5
    z, h = here >> 1, here & 1
    sources = (2 * ((z - 1) & 3) + h, 2 * ((z + 1) & 3) + h, 2 * z + 1 - h)

    def sent(phase, link):
        return table_ref[(row + phase) * 24 + here * LINKS + link]

    def got(phase, link):
        return table_ref[(row + phase) * 24 + sources[link] * LINKS + link]

    return sent, got


def run_copies(copies):
    for begin in (True, False):
        for condition, source, target, sem in copies:
            def act(source=source, target=target, sem=sem):
                copy = pltpu.make_async_copy(source, target, sem)
                if begin:
                    copy.start()
                else:
                    copy.wait()
            if condition is None:
                act()
            else:
                pl.when(condition)(act)


def share_kernel(ids_ref, store_hbm, out_hbm, stage, sems):
    core = lax.axis_index("rel") & 1
    slots = range(2 * PIECES)

    def load(slot):
        stored = piece_of(store_hbm.at[ids_ref[slot // PIECES] & 1], slot % PIECES, 1 - core)
        return pltpu.make_async_copy(stored, stage.at[slot], sems.at[slot])

    def store(slot):
        return pltpu.make_async_copy(stage.at[slot], out_hbm.at[slot], sems.at[slot])

    for slot in slots:
        load(slot).start()
    for slot in slots:
        load(slot).wait()
        store(slot).start()
    for slot in slots:
        store(slot).wait()


def first_kernel(ids_ref, table_ref, store_hbm, shared_hbm, held_hbm, *rest):
    outs, stage, sems = rest[:LINKS], rest[LINKS], rest[LINKS + 1]
    me = lax.axis_index("rel")
    core = me & 1
    sent, _ = plan(ids_ref, table_ref)
    loads, stores = [], []
    for slot in range(2 * PIECES):
        snap = slot // PIECES
        root = ids_ref[snap] >> 1
        here = (root >> 1) == (me >> 1)
        stored = piece_of(store_hbm.at[ids_ref[snap] & 1], slot % PIECES, core)
        loads.append((root == me, stored, stage.at[slot], sems.at[slot]))
        loads.append((root == (me ^ 1), shared_hbm.at[slot], stage.at[slot], sems.at[slot]))
        for link in range(LINKS):
            chosen = jnp.logical_and(here, sent(0, link) == slot)
            stores.append((chosen, stage.at[slot], outs[link], sems.at[2 * PIECES + link]))
        stores.append((here, stage.at[slot], held_hbm.at[slot], sems.at[slot]))
    run_copies(loads)
    run_copies(stores)


def forward_kernel(phase, brought, ids_ref, table_ref, held_in, *rest):
    arrived, held_hbm, outs, stage, sems = (
        rest[:brought], rest[brought], rest[brought + 1 : -2], rest[-2], rest[-1]
    )
    sent, got = plan(ids_ref, table_ref)
    loads, stores = [], []
    for link in range(len(outs)):
        slot = sent(phase, link)
        at = LINKS + link
        older = slot >= 0
        for way in range(brought):
            fresh = jnp.logical_and(slot >= 0, got(phase - 1, way) == slot)
            older = jnp.logical_and(older, got(phase - 1, way) != slot)
            stores.append((fresh, stage.at[way], outs[link], sems.at[at]))
        loads.append((older, held_in.at[jnp.maximum(slot, 0)], stage.at[at], sems.at[at]))
        stores.append((older, stage.at[at], outs[link], sems.at[at]))
    for way in range(brought):
        slot = got(phase - 1, way)
        loads.append((None, arrived[way], stage.at[way], sems.at[way]))
        stores.append((slot >= 0, stage.at[way], held_hbm.at[jnp.maximum(slot, 0)], sems.at[way]))
    run_copies(loads)
    run_copies(stores)


def edge_kernel(held_hbm, out_ref, stage, sems):
    core = lax.axis_index("rel") & 1
    pairs = [(snap, pair) for snap in range(2) for pair in range(2)]
    run_copies([
        (None, held_hbm.at[snap * PIECES + 2 * core + pair, 3], stage.at[snap, pl.ds(2 * pair, 2)], sems.at[2 * snap + pair])
        for snap, pair in pairs
    ])
    rows = stage[...].astype(jnp.float32)
    out_ref[...] = jnp.where(core == 0, rows[:, :, 0], rows[:, :, 15])


def moved(kernel, inputs, scalars, outs, stages, sems, aliases):
    anywhere = pl.BlockSpec(memory_space=pl.ANY)
    smem = pl.BlockSpec(memory_space=pltpu.SMEM)
    return pl.pallas_call(
        kernel,
        out_shape=tuple(jax.ShapeDtypeStruct(shape, jnp.bfloat16) for shape in outs),
        in_specs=[smem] * len(scalars) + [anywhere] * len(inputs),
        out_specs=(anywhere,) * len(outs),
        scratch_shapes=[pltpu.VMEM((stages,) + PIECE, jnp.bfloat16), pltpu.SemaphoreType.DMA((sems,))],
        compiler_params=pltpu.CompilerParams(vmem_limit_bytes=16 * 2**20),
        input_output_aliases=aliases,
        cost_estimate=pl.CostEstimate(flops=0, bytes_accessed=2**21, transcendentals=0),
    )(*scalars, *inputs)


def exchange(sends):
    shifts = ((1, 0), (3, 0), (0, 1))
    arrived = []
    for send, (dz, dh) in zip(sends, shifts):
        pairs = []
        for z in range(4):
            for h in range(2):
                for core in range(2):
                    pairs.append((z * 4 + h * 2 + core, (z + dz) % 4 * 4 + (h ^ dh) * 2 + core))
        arrived.append(lax.ppermute(send, "rel", pairs))
    return arrived


def other_core(value):
    return lax.ppermute(value, "rel", [(i, i ^ 1) for i in range(16)])


def broadcast(wind_store, ids):
    table = jnp.asarray(SCHEDULES, jnp.int32).reshape(-1)
    every = (2 * PIECES,) + PIECE
    (shared,) = moved(share_kernel, (wind_store,), (ids,), (every,), 2 * PIECES, 2 * PIECES, {})
    shared = other_core(shared)
    held, *sends = moved(
        first_kernel, (wind_store, shared), (ids, table), (every,) + (PIECE,) * LINKS,
        2 * PIECES, 2 * PIECES + LINKS, {}
    )

    def forward(phase, held, arrived, links):
        return moved(
            functools.partial(forward_kernel, phase, len(arrived)), (held, *arrived), (ids, table),
            (every,) + (PIECE,) * links, 2 * LINKS, 2 * LINKS, {2: 0},
        )

    for phase in range(1, PHASES):
        held, *sends = forward(phase, held, exchange(sends), LINKS)
    (held,) = forward(PHASES, held, exchange(sends), 0)

    def once_more(held):
        held, *sends = forward(PHASES, held, [], LINKS)
        return forward(PHASES + 1, held, exchange(sends), 0)[0]

    held = lax.cond(ids[0] >> 2 == ids[1] >> 2, once_more, lambda held: held, held)
    edges = pl.pallas_call(
        edge_kernel,
        out_shape=jax.ShapeDtypeStruct((2, 4, 1024), jnp.float32),
        in_specs=[pl.BlockSpec(memory_space=pl.ANY)],
        out_specs=pl.BlockSpec(memory_space=pltpu.VMEM),
        scratch_shapes=[pltpu.VMEM((2, 4, 16, 1024), jnp.bfloat16), pltpu.SemaphoreType.DMA((4,))],
    )(held)
    ends = []
    for flip in range(2):
        pairs = []
        for slab in range(8):
            for rel in range(16):
                to = slab - 1 + 2 * (rel & 1)
                if 0 <= to < 8:
                    pairs.append((slab * 16 + rel, to * 16 + (rel ^ flip)))
        ends.append(lax.ppermute(edges, ("slab", "rel"), pairs))
    even = lax.axis_index("rel") % 2 == 0
    kd_halos = jnp.stack([jnp.where(even, ends[1], ends[0]), jnp.where(even, ends[0], ends[1])], axis=2)
    return held, other_core(held), kd_halos


def shifted_y(here, left, right, lane):
    south_one = pltpu.roll(jnp.where(lane == LANES - 1, left, here), 1, 1)
    south_two = pltpu.roll(jnp.where(lane >= LANES - 2, left, here), 2, 1)
    north_one = pltpu.roll(jnp.where(lane == 0, right, here), LANES - 1, 1)
    north_two = pltpu.roll(jnp.where(lane <= 1, right, here), LANES - 2, 1)
    return south_two, south_one, north_one, north_two


def upwind(courant):
    sixth = courant * (1.0 / 6.0)
    positive = jnp.maximum(sixth, 0.0)
    negative = positive - sixth
    twice = sixth + sixth
    return (
        -positive,
        4.0 * positive + twice,
        4.0 * negative - twice,
        -negative,
        3.0 * (positive + negative),
    )


def step_kernel(
    snap, cells_ref, amount_ref, field_hbm, west_ref, east_ref, mine_hbm, other_hbm, kd_halo_ref,
    out_hbm, west_out, east_out,
    field, result, wind, half_kd, in_sems, wind_sems, out_sems,
):
    releases, levels, chunks, padded_rows, _ = field.shape
    rows = result.shape[3]
    block = 16

    def load(j):
        return pltpu.make_async_copy(
            field_hbm.at[:, :, :, pl.ds(pl.multiple_of(j * LANES, LANES), LANES)],
            field.at[:, :, j, pl.ds(PAD, rows), :],
            in_sems.at[j],
        )

    def store(j):
        return pltpu.make_async_copy(
            result.at[:, :, j],
            out_hbm.at[:, :, :, pl.ds(pl.multiple_of(j * LANES, LANES), LANES)],
            out_sems.at[j],
        )

    core = lax.rem(lax.axis_index("rel"), 2)
    wind_copies = []
    for piece in range(PIECES):
        for number, (source, half) in enumerate(((mine_hbm, core), (other_hbm, 1 - core))):
            wind_copies.append(pltpu.make_async_copy(
                source.at[snap * PIECES + piece],
                piece_of(wind, piece, half),
                wind_sems.at[2 * piece + number],
            ))
    for copy in wind_copies:
        copy.start()
    for j in (chunks - 1, *range(chunks - 1)):
        load(j).start()

    for j in range(chunks):
        span = pl.ds(j * LANES, LANES)
        field[:, :, j, PAD - 2 : PAD, :] = west_ref[:, :, :, span]
        field[:, :, j, PAD + rows : PAD + rows + 2, :] = east_ref[:, :, :, span]
        half_kd[:, j, PAD - 1 : PAD, :] = 0.5 * kd_halo_ref[:, 0:1, span]
        half_kd[:, j, PAD + rows : PAD + rows + 1, :] = 0.5 * kd_halo_ref[:, 1:2, span]
    for copy in wind_copies:
        copy.wait()

    def spread_kd(j, carry):
        span = pl.ds(pl.multiple_of(j * LANES, LANES), LANES)
        for level in range(levels):
            half_kd[level, j, PAD : PAD + rows, :] = 0.5 * wind[3, level, :, span].astype(jnp.float32)
        return carry

    lax.fori_loop(0, chunks, spread_kd, 0)
    load(chunks - 1).wait()
    load(0).wait()
    load(1).wait()

    lane = lax.broadcasted_iota(jnp.int32, (block, LANES), 1)
    lane_row = lax.broadcasted_iota(jnp.int32, (1, LANES), 1)

    def chunk(j, carry):
        @pl.when(jnp.logical_and(j > 0, j < chunks - 2))
        def _():
            load(j + 1).wait()

        before = lax.rem(j + chunks - 1, chunks)
        after = lax.rem(j + 1, chunks)
        span = pl.ds(pl.multiple_of(j * LANES, LANES), LANES)

        def rows_block(start):
            here = pl.ds(PAD + start, block)
            kd_here = [half_kd[level, j, here, :] for level in range(levels)]
            for level in range(levels):
                cx = wind[0, level, pl.ds(start, block), span].astype(jnp.float32)
                cy = wind[1, level, pl.ds(start, block), span].astype(jnp.float32)
                cz = wind[2, level, pl.ds(start, block), span].astype(jnp.float32)
                middle_kd = kd_here[level]
                kd_west = middle_kd + half_kd[level, j, pl.ds(PAD + start - 1, block), :]
                kd_east = middle_kd + half_kd[level, j, pl.ds(PAD + start + 1, block), :]
                kd_left = half_kd[level, before, here, :]
                kd_right = half_kd[level, after, here, :]
                kd_south = middle_kd + pltpu.roll(jnp.where(lane == LANES - 1, kd_left, middle_kd), 1, 1)
                kd_north = middle_kd + pltpu.roll(jnp.where(lane == 0, kd_right, middle_kd), LANES - 1, 1)
                kd_below = middle_kd + kd_here[max(level - 1, 0)]
                kd_above = middle_kd + kd_here[min(level + 1, levels - 1)]
                w2, w1, e1, e2, loss_x = upwind(cx)
                s2, s1, n1, n2, loss_y = upwind(cy)
                b2, b1, a1, a2, loss_z = upwind(cz)
                w1, e1 = w1 + kd_west, e1 + kd_east
                s1, n1 = s1 + kd_south, n1 + kd_north
                b1, a1 = b1 + kd_below, a1 + kd_above
                loss = loss_x + loss_y + loss_z
                loss = loss + ((kd_west + kd_east) + (kd_south + kd_north) + (kd_below + kd_above))
                by_level = [None] * levels
                by_level[level] = 1.0 - loss
                for offset, weight in ((-2, b2), (-1, b1), (1, a1), (2, a2)):
                    at = min(max(level + offset, 0), levels - 1)
                    by_level[at] = weight if by_level[at] is None else by_level[at] + weight
                for release in range(releases):
                    center = field[release, level, j, here, :]
                    left = field[release, level, before, here, :]
                    right = field[release, level, after, here, :]
                    south_two, south_one, north_one, north_two = shifted_y(center, left, right, lane)
                    total = by_level[level] * center
                    total = total + (s2 * south_two + s1 * south_one)
                    total = total + (n1 * north_one + n2 * north_two)
                    total = total + (
                        w2 * field[release, level, j, pl.ds(PAD + start - 2, block), :]
                        + w1 * field[release, level, j, pl.ds(PAD + start - 1, block), :]
                    )
                    total = total + (
                        e1 * field[release, level, j, pl.ds(PAD + start + 1, block), :]
                        + e2 * field[release, level, j, pl.ds(PAD + start + 2, block), :]
                    )
                    for other in range(levels):
                        if other != level and by_level[other] is not None:
                            total = total + by_level[other] * field[release, other, j, here, :]
                    result[release, level, j, pl.ds(start, block), :] = total

        for start in range(0, rows, block):
            rows_block(start)

        for release in range(releases):
            at_level = cells_ref[release, 0]
            at_row = cells_ref[release, 1]
            at_y = cells_ref[release, 2]
            spot = (release, at_level, j, pl.ds(at_row, 1), slice(None))
            put = jnp.where(j * LANES + lane_row == at_y, amount_ref[release], 0.0)
            result[spot] = result[spot] + put
        west_out[:, :, :, span] = result[:, :, j, 0:2, :]
        east_out[:, :, :, span] = result[:, :, j, rows - 2 : rows, :]
        store(j).start()
        return carry

    lax.fori_loop(0, chunks, chunk, 0)
    for j in range(chunks):
        store(j).wait()


def step(snap, field, west, east, mine, other, kd_halo, cells, amounts):
    releases, levels, rows, width = field.shape
    chunks = width // LANES
    edge = jax.ShapeDtypeStruct((releases, levels, 2, width), jnp.float32)
    vmem = pl.BlockSpec(memory_space=pltpu.VMEM)
    smem = pl.BlockSpec(memory_space=pltpu.SMEM)
    anywhere = pl.BlockSpec(memory_space=pl.ANY)
    return pl.pallas_call(
        functools.partial(step_kernel, snap),
        out_shape=(jax.ShapeDtypeStruct(field.shape, jnp.float32), edge, edge),
        in_specs=[smem, smem, anywhere, vmem, vmem, anywhere, anywhere, vmem],
        out_specs=(anywhere, vmem, vmem),
        scratch_shapes=[
            pltpu.VMEM((releases, levels, chunks, rows + 2 * PAD, LANES), jnp.float32),
            pltpu.VMEM((releases, levels, chunks, rows, LANES), jnp.float32),
            pltpu.VMEM((4, levels, rows, width), jnp.bfloat16),
            pltpu.VMEM((levels, chunks, rows + 2 * PAD, LANES), jnp.float32),
            pltpu.SemaphoreType.DMA((chunks,)),
            pltpu.SemaphoreType.DMA((2 * PIECES,)),
            pltpu.SemaphoreType.DMA((chunks,)),
        ],
        compiler_params=pltpu.CompilerParams(vmem_limit_bytes=40 * 2**20),
        cost_estimate=pl.CostEstimate(flops=60 * field.size, bytes_accessed=12 * field.size, transcendentals=0),
    )(cells, amounts, field, west, east, mine, other, kd_halo)


def halos(first, last):
    count = lax.axis_size("slab")
    up = [(i, (i + 1) % count) for i in range(count - 1)]
    down = [(j, i) for i, j in up]
    return lax.ppermute(last, "slab", up), lax.ppermute(first, "slab", down)


def body(concentration, wind_store, sources, emission, snapshot_ids):
    slab_cells = concentration.shape[2]
    width_y = concentration.shape[3]
    full_x = slab_cells * lax.axis_size("slab")
    offset = lax.axis_index("slab") * slab_cells
    local_x = sources // width_y % full_x - offset
    owned = jnp.logical_and(local_x >= 0, local_x < slab_cells)
    amounts = jnp.where(owned, emission, jnp.zeros_like(emission))
    cells = jnp.stack(
        [sources // (full_x * width_y), jnp.clip(local_x, 0, slab_cells - 1), sources % width_y], axis=1
    )
    field = concentration
    west, east = halos(field[:, :, :2], field[:, :, -2:])
    mine, other, kd_halos = broadcast(wind_store, snapshot_ids)
    for number in range(snapshot_ids.shape[0]):
        field, first, last = step(number, field, west, east, mine, other, kd_halos[number], cells, amounts)
        if number + 1 < snapshot_ids.shape[0]:
            west, east = halos(first, last)
    return field


def solution(mesh):
    placed = (
        P("rel", None, "slab", None),
        P("rel", None, None, "slab", None),
        P("rel"),
        P("rel"),
        P(),
    )
    return jax.shard_map(
        body, mesh=mesh, in_specs=placed, out_specs=P("rel", None, "slab", None), check_vma=False
    )
```

```python
import functools
import math
import jax
import jax.numpy as jnp
from jax import lax
from jax.experimental import pallas as pl
from jax.experimental.pallas import tpu as pltpu
from jax.sharding import PartitionSpec as P

LANES = 128
PAD = 16


PIECES = 4
PIECE = (4, 2, 16, 1024)
LINKS = 3
PHASES = 4

SCHEDULES = (
    (
        (2, 4, 5, -1, -1, -1, -1, -1, -1, -1, -1, -1, -1, -1, -1, -1, -1, -1, -1, -1, -1, -1, -1, -1),
        (3, 7, 6, 5, 5, -1, 2, -1, 2, -1, -1, -1, -1, -1, -1, -1, -1, -1, -1, -1, 4, -1, -1, -1),
        (7, 1, 0, 6, 6, -1, 3, -1, 3, 5, -1, 5, 2, -1, 2, -1, -1, -1, 7, 4, 7, -1, 4, 5),
        (1, 0, 1, 0, 0, 0, 7, 2, 7, -1, 3, 6, 3, -1, 3, 2, -1, 5, -1, 1, -1, 4, 6, -1),
        (7, 7, 7, 4, 1, 5, 3, 6, 1, 0, 0, 0, 1, 4, 1, 3, 6, 6, 4, 0, 5, 2, 7, 6),
    ),
    (
        (-1, -1, -1, -1, -1, -1, -1, -1, -1, -1, -1, -1, -1, -1, -1, -1, -1, -1, -1, -1, -1, -1, -1, -1),
        (0, 3, 1, 5, 7, 6, -1, -1, -1, -1, -1, -1, -1, -1, -1, -1, -1, -1, -1, -1, -1, -1, -1, -1),
        (1, 2, 2, 4, 6, 4, 0, -1, 0, 5, -1, 5, -1, -1, -1, -1, -1, -1, -1, 3, 3, -1, 7, 7),
        (6, 4, 3, 2, 1, -1, 1, -1, -1, 4, 5, 4, 3, 3, 0, 5, 7, 7, 7, 2, 2, 6, 6, 6),
        (7, 0, 1, 1, 7, 5, 5, 6, 3, 2, 0, 2, 1, 1, 1, 0, 6, 6, 4, 4, 4, 2, 3, 5),
    ),
    (
        (-1, -1, -1, -1, -1, -1, -1, -1, -1, -1, -1, -1, -1, -1, -1, -1, -1, -1, -1, -1, -1, -1, -1, -1),
        (0, 3, 0, -1, -1, -1, 6, 5, 7, -1, -1, -1, -1, -1, -1, -1, -1, -1, -1, -1, -1, -1, -1, -1),
        (1, 2, 1, -1, 0, -1, 4, 7, 5, 7, 7, -1, 6, -1, 6, -1, -1, -1, -1, 3, 3, -1, -1, -1),
        (2, 5, 2, 0, 7, 1, 1, 4, 1, 5, 5, -1, 4, 3, 4, 6, 6, 7, -1, 6, 2, 3, 0, 0),
        (7, 7, 4, 2, 1, 5, 2, 6, 3, 1, 0, 0, 1, 4, 3, 5, 4, 5, 4, 0, 4, 6, 2, -1),
    ),
    (
        (-1, -1, -1, -1, -1, -1, -1, -1, -1, -1, -1, -1, -1, -1, -1, -1, -1, -1, -1, -1, -1, -1, -1, -1),
        (0, 2, 1, -1, -1, -1, -1, -1, -1, 6, 4, 5, -1, -1, -1, -1, -1, -1, -1, -1, -1, -1, -1, -1),
        (3, 3, 0, 1, 1, 4, 0, 5, 0, 4, 5, 7, -1, -1, -1, -1, -1, 6, -1, 2, 2, -1, -1, -1),
        (1, 5, 3, -1, 0, -1, 7, 7, 3, 5, 7, 6, 6, 2, 2, 4, 4, 4, -1, -1, 3, -1, 1, 1),
        (7, 7, 1, 7, 7, 5, 1, 6, 3, 3, 6, 0, 0, 4, 7, 5, 2, 5, -1, 3, 6, 2, 0, 4),
    ),
    (
        (-1, -1, -1, -1, -1, -1, -1, -1, -1, -1, -1, -1, -1, -1, -1, -1, -1, -1, -1, -1, -1, -1, -1, -1),
        (0, 2, 3, -1, -1, -1, -1, -1, -1, -1, -1, -1, 6, 7, 5, -1, -1, -1, -1, -1, -1, -1, -1, -1),
        (1, 1, 1, 3, 3, -1, 0, 7, 0, -1, -1, -1, 4, 6, 4, -1, 5, -1, -1, 2, 6, -1, -1, -1),
        (3, 3, 7, 1, 1, 1, 1, 0, 6, 0, 5, -1, 5, 2, 2, 4, 4, -1, 2, 4, 2, 6, 3, 6),
        (7, 7, 0, 7, 7, 5, 6, 6, 3, 6, 4, 5, 0, 4, 7, 0, 2, 5, 4, 3, 5, 2, 1, 2),
    ),
    (
        (-1, -1, -1, -1, -1, -1, -1, -1, -1, -1, -1, -1, -1, -1, -1, -1, -1, -1, -1, -1, -1, -1, -1, -1),
        (1, 3, 0, -1, -1, -1, -1, -1, -1, -1, -1, -1, -1, -1, -1, 7, 5, 4, -1, -1, -1, -1, -1, -1),
        (0, 2, 1, -1, 0, -1, 1, -1, -1, -1, -1, 5, 4, -1, -1, 5, 6, 6, -1, 3, -1, 7, 7, 7),
        (2, 3, 3, 1, 1, 7, 0, 5, 0, 6, 6, 6, 6, 3, 3, 4, 4, 7, 4, 2, 2, 5, 0, 0),
        (7, 5, 4, 7, 3, 5, 6, 6, 2, 1, 0, 4, 1, 1, 7, 5, 3, 5, 4, 3, 6, 2, 2, 2),
    ),
    (
        (-1, -1, -1, -1, -1, -1, -1, -1, -1, -1, -1, -1, -1, -1, -1, -1, -1, -1, -1, -1, -1, -1, -1, -1),
        (0, 1, 1, -1, -1, -1, -1, -1, -1, -1, -1, -1, -1, -1, -1, -1, -1, -1, 6, 5, 7, -1, -1, -1),
        (2, 3, 6, 1, -1, -1, 0, -1, 0, -1, -1, -1, -1, -1, 5, -1, -1, -1, 7, 4, 4, 7, 7, -1),
        (3, 7, 2, 6, 6, -1, 2, 0, 2, 1, -1, 1, 0, 4, 0, 5, 5, 7, -1, 1, 3, 4, 4, -1),
        (6, 3, 3, 7, 2, 4, 3, -1, 3, 6, 0, 5, 2, 7, 2, 1, 4, -1, 5, 6, 0, 5, 3, 4),
    ),
    (
        (-1, -1, -1, -1, -1, -1, -1, -1, -1, -1, -1, -1, -1, -1, -1, -1, -1, -1, -1, -1, -1, -1, -1, -1),
        (3, 1, 2, -1, -1, -1, -1, -1, -1, -1, -1, -1, -1, -1, -1, -1, -1, -1, -1, -1, -1, 5, 6, 7),
        (0, 3, 0, 2, 2, 5, 3, -1, 3, -1, -1, -1, -1, -1, -1, -1, 6, 6, 7, 1, -1, 4, 4, 4),
        (2, 5, 1, 5, 0, 0, -1, 3, 0, 2, 6, 6, 1, 1, 1, -1, -1, 4, 4, 7, 3, 7, 5, 2),
        (7, 0, 3, 7, 7, 5, 0, 6, 1, 3, 0, 5, -1, 4, 7, 1, 4, 5, 4, 2, 5, 2, 0, 6),
    ),
)


def piece_of(tile, piece, half):
    at = pl.multiple_of(half * 32 + 16 * (piece // 2), 16)
    return tile.at[:, pl.ds(2 * (piece % 2), 2), pl.ds(at, 16), :]


def plan(ids_ref, table_ref):
    chip = lax.axis_index("rel") >> 1
    first = ids_ref[0] >> 2
    second = ids_ref[1] >> 2

    def place(of):
        return 2 * (((of >> 1) - (first >> 1)) & 3) + ((of ^ first) & 1)

    here = place(chip)
    row = place(second) * 5
    z, h = here >> 1, here & 1
    sources = (2 * ((z - 1) & 3) + h, 2 * ((z + 1) & 3) + h, 2 * z + 1 - h)

    def sent(phase, link):
        return table_ref[(row + phase) * 24 + here * LINKS + link]

    def got(phase, link):
        return table_ref[(row + phase) * 24 + sources[link] * LINKS + link]

    return sent, got


def run_copies(copies, stages=(True, False)):
    for begin in stages:
        for condition, source, target, sem in copies:
            def act(source=source, target=target, sem=sem):
                copy = pltpu.make_async_copy(source, target, sem)
                if begin:
                    copy.start()
                else:
                    copy.wait()
            if condition is None:
                act()
            else:
                pl.when(condition)(act)


def run_staged(loads, stores):
    run_copies(loads)
    run_copies(stores)


def share_kernel(ids_ref, store_ref, out_ref, stage, sems):
    core = lax.axis_index("rel") & 1
    slots = range(2 * PIECES)
    run_staged(
        [
            (None, piece_of(store_ref.at[ids_ref[slot // PIECES] & 1], slot % PIECES, 1 - core), stage.at[slot], sems.at[slot])
            for slot in slots
        ],
        [(None, stage.at[slot], out_ref.at[slot], sems.at[slot]) for slot in slots],
    )


def first_kernel(phase, brought, keeps, ids_ref, table_ref, store_ref, shared_ref, *rest):
    arrived, outs, held_ref = rest[:brought], rest[brought : brought + LINKS], rest[brought + LINKS]
    stage, sems = rest[-2:]
    me = lax.axis_index("rel")
    core = me & 1
    sent, got = plan(ids_ref, table_ref)
    loads, stores = [], []
    for slot in range(2 * PIECES):
        root = ids_ref[slot // PIECES] >> 1
        stored = piece_of(store_ref.at[ids_ref[slot // PIECES] & 1], slot % PIECES, core)
        loads.append((root == me, stored, stage.at[slot], sems.at[slot]))
        loads.append((root == (me ^ 1), shared_ref.at[slot], stage.at[slot], sems.at[slot]))
        held = (root >> 1) == (me >> 1)
        for link in range(LINKS):
            chosen = jnp.logical_and(held, sent(phase, link) == slot)
            stores.append((chosen, stage.at[slot], outs[link], sems.at[link]))
        if keeps:
            stores.append((held, stage.at[slot], held_ref.at[slot], sems.at[2 * LINKS + slot]))
    for way in range(brought):
        slot = got(0, way)
        at = 2 * PIECES + way
        loads.append((None, arrived[way], stage.at[at], sems.at[at]))
        for link in range(LINKS):
            chosen = jnp.logical_and(slot >= 0, sent(phase, link) == slot)
            stores.append((chosen, stage.at[at], outs[link], sems.at[link]))
        stores.append((slot >= 0, stage.at[at], held_ref.at[jnp.maximum(slot, 0)], sems.at[LINKS + way]))
    run_staged(loads, stores)


def forward_kernel(phase, ids_ref, table_ref, *rest):
    arrived, held_ref, outs, stage, sems = rest[:LINKS], rest[LINKS], rest[LINKS + 1 : -2], rest[-2], rest[-1]
    sent, got = plan(ids_ref, table_ref)
    loads, stores = [], []
    for link in range(LINKS):
        slot = sent(phase + 1, link)
        loads.extend(
            (condition, source, stage.at[link], sems.at[link])
            for condition, source in wherever(slot, phase, got, arrived, held_ref)
        )
        stores.append((slot >= 0, stage.at[link], outs[link], sems.at[link]))
    run_staged(loads, stores)


def keep_kernel(phase, ids_ref, table_ref, *rest):
    arrived, held_ref, stage, sems = rest[:LINKS], *rest[LINKS + 1 :]
    _, got = plan(ids_ref, table_ref)
    ways = range(LINKS)
    run_staged(
        [(got(phase, way) >= 0, arrived[way], stage.at[way], sems.at[way]) for way in ways],
        [(got(phase, way) >= 0, stage.at[way], held_ref.at[jnp.maximum(got(phase, way), 0)], sems.at[way]) for way in ways],
    )


def wherever(slot, phase, got, arrived, held_ref, inner=()):
    older = slot >= 0
    places = []
    for way in range(LINKS):
        places.append((jnp.logical_and(slot >= 0, got(phase, way) == slot), arrived[way].at[inner] if inner else arrived[way]))
        older = jnp.logical_and(older, got(phase, way) != slot)
    return [*places, (older, held_ref.at[(jnp.maximum(slot, 0), *inner)])]


def edge_kernel(ids_ref, table_ref, *rest):
    arrived, held_ref, out_ref, last_ref, stage, stage_kd, rows, last, sems = rest[:LINKS], *rest[LINKS:]
    core = lax.axis_index("rel") & 1
    _, got = plan(ids_ref, table_ref)
    copies = []
    for pair in range(2):
        slot = 2 * core + pair
        for condition, source in wherever(slot, PHASES, got, arrived, held_ref):
            copies.append((condition, source, stage.at[pair], sems.at[pair]))
        for condition, source in wherever(PIECES + slot, PHASES, got, arrived, held_ref, (3,)):
            copies.append((condition, source, stage_kd.at[pair], sems.at[2 + pair]))
    for way in range(LINKS):
        copies.append((None, arrived[way], last.at[way], sems.at[4 + way]))
    run_copies(copies)
    out_copies = [(None, last, last_ref, sems.at[4])]
    run_copies(out_copies, (True,))
    rows[:, 10:, :] = jnp.zeros_like(rows[:, 10:, :])
    for level in range(4):
        def ends(block, count):
            block = block.astype(jnp.float32)
            return jnp.where(core == 0, block[:count], block[16 - count :])

        for channel in range(3):
            rows[level, 2 * channel : 2 * channel + 2, :] = ends(stage[level // 2, channel, level % 2], 2)
        rows[level, 6:9, :] = ends(stage[level // 2, 3, level % 2], 3)
        rows[level, 9:10, :] = ends(stage_kd[level // 2, level % 2], 1)
    out_ref[...] = rows[...].astype(jnp.bfloat16)
    run_copies(out_copies, (False,))


def moved(kernel, scalars, inputs, outs, scratch, aliases=None, vmem_outs=0):
    smem = pl.BlockSpec(memory_space=pltpu.SMEM)
    anywhere = pl.BlockSpec(memory_space=pl.ANY)
    return pl.pallas_call(
        kernel,
        out_shape=tuple(jax.ShapeDtypeStruct(shape, jnp.bfloat16) for shape in outs),
        in_specs=[smem] * len(scalars) + [anywhere] * len(inputs),
        out_specs=(pl.BlockSpec(memory_space=pltpu.VMEM),) * vmem_outs + (anywhere,) * (len(outs) - vmem_outs),
        scratch_shapes=scratch,
        input_output_aliases=aliases or {},
        compiler_params=pltpu.CompilerParams(vmem_limit_bytes=12 * 2**20),
        cost_estimate=pl.CostEstimate(flops=0, bytes_accessed=2**21, transcendentals=0),
    )(*scalars, *inputs)


def exchange(sends):
    shifts = ((1, 0), (3, 0), (0, 1))
    arrived = []
    for send, (dz, dh) in zip(sends, shifts):
        pairs = []
        for z in range(4):
            for h in range(2):
                for core in range(2):
                    pairs.append((z * 4 + h * 2 + core, (z + dz) % 4 * 4 + (h ^ dh) * 2 + core))
        arrived.append(lax.ppermute(send, "rel", pairs))
    return arrived


def other_core(value):
    return lax.ppermute(value, "rel", [(i, i ^ 1) for i in range(16)])


def broadcast(wind_store, ids, field):
    table = jnp.asarray(SCHEDULES, jnp.int32).reshape(-1)
    every = (2 * PIECES,) + PIECE
    dma = pltpu.SemaphoreType.DMA
    sent = [PIECE] * LINKS

    def stage(slots):
        return pltpu.VMEM((slots,) + PIECE, jnp.bfloat16)

    (shared,) = moved(share_kernel, (ids,), [wind_store], [every], [stage(2 * PIECES), dma((2 * PIECES,))])
    shared = other_core(shared)

    def begin(phase, keeps, wind_store, shared, arrived):
        return moved(
            functools.partial(first_kernel, phase, len(arrived), keeps), (ids, table), [wind_store, shared, *arrived],
            sent + [every] * keeps, [stage(2 * PIECES + LINKS), dma((2 * LINKS + 2 * PIECES,))],
        )

    def one_chip(wind_store, shared):
        return begin(1, True, wind_store, shared, exchange(begin(0, False, wind_store, shared, [])))

    *sends, held = lax.cond(
        ids[0] >> 2 == ids[1] >> 2, one_chip, lambda store, shared: begin(1, True, store, shared, []), wind_store, shared
    )
    ends = (field[:, :, :4], field[:, :, -4:])
    for phase in range(1, PHASES + 1):
        if phase == 2:
            *ends, sends[0] = lax.optimization_barrier((*ends, sends[0]))
            west, east = halos(*ends)
        arrived = exchange(sends)
        if phase == 3:
            west, east, arrived[0] = lax.optimization_barrier((west, east, arrived[0]))
        if phase < PHASES:
            sends = moved(
                functools.partial(forward_kernel, phase), (ids, table), [*arrived, held], sent, [stage(LINKS), dma((LINKS,))]
            )
            *sends, held = lax.optimization_barrier((*sends, held))
            (held,) = moved(
                functools.partial(keep_kernel, phase), (ids, table), [*arrived, held], [every], [stage(LINKS), dma((LINKS,))],
                {2 + LINKS: 0},
            )
    other = other_core(held)
    other, arrived[0] = lax.optimization_barrier((other, arrived[0]))
    edges, last = moved(
        edge_kernel, (ids, table), [*arrived, held], [(4, 16, 1024), (LINKS,) + PIECE],
        [
            stage(2), pltpu.VMEM((2,) + PIECE[1:], jnp.bfloat16), pltpu.VMEM((4, 16, 1024), jnp.float32), stage(LINKS),
            dma((4 + LINKS,)),
        ], vmem_outs=1,
    )
    ends = []
    for flip in range(2):
        pairs = []
        for slab in range(8):
            for rel in range(16):
                to = slab - 1 + 2 * (rel & 1)
                if 0 <= to < 8:
                    pairs.append((slab * 16 + rel, to * 16 + (rel ^ flip)))
        ends.append(lax.ppermute(edges, ("slab", "rel"), pairs))
    after, west, east, edges = lax.optimization_barrier((field, west, east, edges))
    start = lay_out(after, west, east)
    return (ids, table), start, held, other, last, other_core(last), *ends


def shifted_y(here, left, right, lane):
    south_one = pltpu.roll(jnp.where(lane == LANES - 1, left, here), 1, 1)
    south_two = pltpu.roll(jnp.where(lane >= LANES - 2, left, here), 2, 1)
    north_one = pltpu.roll(jnp.where(lane == 0, right, here), LANES - 1, 1)
    north_two = pltpu.roll(jnp.where(lane <= 1, right, here), LANES - 2, 1)
    return south_two, south_one, north_one, north_two


def upwind(courant):
    sixth = courant * (1.0 / 6.0)
    far = jnp.abs(sixth)
    near = far + far
    tilt = 4.0 * sixth
    return near + tilt, near - tilt, far


def roll_one(here, left, right, lane):
    south = pltpu.roll(jnp.where(lane == LANES - 1, left, here), 1, 1)
    north = pltpu.roll(jnp.where(lane == 0, right, here), LANES - 1, 1)
    return south, north


def weights(level, levels, cx, cy, cz, kd_here, kd_west, kd_east, kd_left, kd_right, lane):
    middle = kd_here[level]
    kd_south, kd_north = roll_one(middle, kd_left, kd_right, lane)
    west, east = middle + kd_west, middle + kd_east
    south, north = middle + kd_south, middle + kd_north
    below = middle + kd_here[max(level - 1, 0)]
    above = middle + kd_here[min(level + 1, levels - 1)]
    w1, e1, far_x = upwind(cx)
    s1, n1, far_y = upwind(cy)
    b1, a1, far_z = upwind(cz)
    loss = 3.0 * (far_x + far_y + far_z) + ((west + east) + (south + north) + (below + above))
    positive = jnp.maximum(cz * (1.0 / 6.0), 0.0)
    by_level = [None] * levels
    by_level[level] = 1.0 - loss
    for offset, weight in ((-2, -positive), (-1, b1 + below), (1, a1 + above), (2, positive - far_z)):
        at = min(max(level + offset, 0), levels - 1)
        by_level[at] = weight if by_level[at] is None else by_level[at] + weight
    return (cx > 0.0, far_x, w1 + west, e1 + east), (cy > 0.0, far_y, s1 + south, n1 + north), by_level


def weighted(along_x, along_y, by_level, level, x_cells, columns, left, right, lane):
    center = columns[level]
    y_cells = shifted_y(center, left, right, lane)
    total = by_level[level] * center
    for (forward, far, behind, ahead), cells in ((along_y, y_cells), (along_x, x_cells)):
        total = total + (behind * cells[1] + ahead * cells[2])
        total = total - far * jnp.where(forward, cells[0], cells[3])
    for other, weight in enumerate(by_level):
        if other != level and weight is not None:
            total = total + weight * columns[other]
    return total


def lay_out_kernel(field_hbm, west_ref, east_ref, out_ref, sems):
    chunks = out_ref.shape[2]
    rows = out_ref.shape[3] - 2 * PAD
    copies = []
    for j in range(chunks):
        span = pl.ds(j * LANES, LANES)
        copies.append((None, field_hbm.at[:, :, :, span], out_ref.at[:, :, j, pl.ds(PAD, rows), :], sems.at[j]))
        out_ref[:, :, j, PAD - 4 : PAD, :] = west_ref[:, :, :, span]
        out_ref[:, :, j, PAD + rows : PAD + rows + 4, :] = east_ref[:, :, :, span]
    run_copies(copies)


def lay_out(field, west, east):
    releases, levels, rows, width = field.shape
    chunks = width // LANES
    vmem = pl.BlockSpec(memory_space=pltpu.VMEM)
    return pl.pallas_call(
        lay_out_kernel,
        out_shape=jax.ShapeDtypeStruct((releases, levels, chunks, rows + 2 * PAD, LANES), jnp.float32),
        in_specs=[pl.BlockSpec(memory_space=pltpu.HBM), vmem, vmem],
        out_specs=vmem,
        scratch_shapes=[pltpu.SemaphoreType.DMA((chunks,))],
        compiler_params=pltpu.CompilerParams(vmem_limit_bytes=16 * 2**20),
        cost_estimate=pl.CostEstimate(flops=0, bytes_accessed=2**23, transcendentals=0),
    )(field, west, east)


def steps_kernel(ids_ref, table_ref, cells_ref, amount_ref, first, mine_ref, other_ref, mine_last, other_last, *rest):
    near_ref, far_ref, out_hbm, second, result, winds, half_kds, halo_wind, wind_sems, out_sems = rest
    releases, levels, chunks, padded_rows, _ = first.shape
    rows = padded_rows - 2 * PAD
    core = lax.rem(lax.axis_index("rel"), 2)
    slab = lax.axis_index("slab")

    def store(j):
        return pltpu.make_async_copy(
            result.at[:, :, j],
            out_hbm.at[:, :, :, pl.ds(pl.multiple_of(j * LANES, LANES), LANES)],
            out_sems.at[j],
        )

    _, got = plan(ids_ref, table_ref)
    wind_copies = []
    for slot in range(2 * PIECES):
        for number, (held_ref, last, half) in enumerate(((mine_ref, mine_last, core), (other_ref, other_last, 1 - core))):
            target = piece_of(winds.at[slot // PIECES], slot % PIECES, half)
            for condition, source in wherever(jnp.int32(slot), PHASES, got, [last.at[way] for way in range(LINKS)], held_ref):
                wind_copies.append((condition, source, target, wind_sems.at[2 * slot + number]))
    run_copies(wind_copies, (True,))

    lane = lax.broadcasted_iota(jnp.int32, (8, LANES), 1)
    sublane = lax.broadcasted_iota(jnp.int32, (8, LANES), 0)
    lane_row = lax.broadcasted_iota(jnp.int32, (1, LANES), 1)

    def span_of(j):
        return pl.ds(pl.multiple_of(j * LANES, LANES), LANES)

    def halo_rows(j, carry):
        span = span_of(j)
        near = near_ref[:, :, span].astype(jnp.float32)
        far = far_ref[:, :, span].astype(jnp.float32)
        east = jnp.where(core == 0, near, far)
        west = jnp.where(core == 0, far, near)
        for channel in range(3):
            halo_wind[channel, :, j, 0:2, :] = east[:, 2 * channel : 2 * channel + 2]
            halo_wind[channel, :, j, 6:8, :] = west[:, 2 * channel : 2 * channel + 2]
        half_kds[0, :, j, PAD + rows : PAD + rows + 3, :] = 0.5 * east[:, 6:9]
        half_kds[0, :, j, PAD - 3 : PAD, :] = 0.5 * west[:, 6:9]
        half_kds[1, :, j, PAD + rows : PAD + rows + 1, :] = 0.5 * east[:, 9:10]
        half_kds[1, :, j, PAD - 1 : PAD, :] = 0.5 * west[:, 9:10]
        return carry

    lax.fori_loop(0, chunks, halo_rows, 0)
    run_copies(wind_copies, (False,))

    def spread_kd(j, carry):
        for snap in range(2):
            for level in range(levels):
                half_kds[snap, level, j, PAD : PAD + rows, :] = 0.5 * winds[snap, 3, level, :, span_of(j)].astype(jnp.float32)
        return carry

    lax.fori_loop(0, chunks, spread_kd, 0)

    def chunk(snap, source, target, pad, j):
        before = lax.rem(j + chunks - 1, chunks)
        after = lax.rem(j + 1, chunks)
        span = span_of(j)
        half_kd = half_kds.at[snap]

        for start in range(0, rows, 16):
            for level in range(levels):
                courant = [
                    winds[snap, channel, level, pl.ds(start, 16), span].astype(jnp.float32) for channel in range(3)
                ]
                for half in range(2):
                    at = PAD + start + 8 * half
                    here = pl.ds(at, 8)
                    cx, cy, cz = (value[8 * half : 8 * half + 8] for value in courant)
                    along_x, along_y, by_level = weights(
                        level, levels, cx, cy, cz,
                        [half_kd[other, j, here, :] for other in range(levels)],
                        half_kd[level, j, pl.ds(at - 1, 8), :], half_kd[level, j, pl.ds(at + 1, 8), :],
                        half_kd[level, before, here, :], half_kd[level, after, here, :], lane,
                    )
                    for release in range(releases):
                        target[release, level, j, pl.ds(at - PAD + pad, 8), :] = weighted(
                            along_x, along_y, by_level, level,
                            [source[release, level, j, pl.ds(at + shift, 8), :] for shift in (-2, -1, 1, 2)],
                            [source[release, other, j, here, :] for other in range(levels)],
                            source[release, level, before, here, :], source[release, level, after, here, :], lane,
                        )

    def halo_chunk(j):
        before = lax.rem(j + chunks - 1, chunks)
        after = lax.rem(j + 1, chunks)
        kept = jnp.logical_or(
            jnp.logical_and(sublane < 4, slab < lax.axis_size("slab") - 1), jnp.logical_and(sublane >= 4, slab > 0)
        )

        def around(ref, index, shift=0):
            east = ref[(*index, pl.ds(PAD + rows + shift, 8), slice(None))]
            west = ref[(*index, pl.ds(PAD - 8 + shift, 8), slice(None))]
            return jnp.where(sublane < 4, east, west)

        half_kd = half_kds.at[0]
        for level in range(levels):
            along_x, along_y, by_level = weights(
                level, levels, *(halo_wind[channel, level, j] for channel in range(3)),
                [around(half_kd, (other, j)) for other in range(levels)],
                around(half_kd, (level, j), -1), around(half_kd, (level, j), 1),
                around(half_kd, (level, before)), around(half_kd, (level, after)), lane,
            )
            for release in range(releases):
                value = weighted(
                    along_x, along_y, by_level, level,
                    [around(first, (release, level, j), shift) for shift in (-2, -1, 1, 2)],
                    [around(first, (release, other, j)) for other in range(levels)],
                    around(first, (release, level, before)), around(first, (release, level, after)), lane,
                )
                value = jnp.where(kept, value, 0.0)
                second[release, level, j, PAD + rows : PAD + rows + 4, :] = value[0:4]
                second[release, level, j, PAD - 4 : PAD, :] = value[4:8]

    def emit(ref, j, pad, reach):
        for release in range(releases):
            at_row = cells_ref[1, release]
            inside = jnp.logical_and(at_row >= -reach, at_row < rows + reach)
            amount = jnp.where(inside, amount_ref[release], 0.0)
            row = pad + jnp.clip(at_row, -reach, rows + reach - 1)
            spot = (release, cells_ref[0, release], j, pl.ds(row, 1), slice(None))
            ref[spot] = ref[spot] + jnp.where(j * LANES + lane_row == cells_ref[2, release], amount, 0.0)

    def first_step(j, carry):
        chunk(0, first, second, PAD, j)
        halo_chunk(j)
        emit(second, j, PAD, 2)
        return carry

    def second_step(j, carry):
        chunk(1, second, result, 0, j)
        emit(result, j, 0, 0)
        store(j).start()
        return carry

    lax.fori_loop(0, chunks, first_step, 0)
    lax.fori_loop(0, chunks, second_step, 0)
    for j in range(chunks):
        store(j).wait()


def steps(shape, scalars, start, mine, other, mine_last, other_last, near, far, cells, amounts):
    releases, levels, rows, width = shape
    chunks = width // LANES
    vmem = pl.BlockSpec(memory_space=pltpu.VMEM)
    smem = pl.BlockSpec(memory_space=pltpu.SMEM)
    anywhere = pl.BlockSpec(memory_space=pl.ANY)
    return pl.pallas_call(
        steps_kernel,
        out_shape=jax.ShapeDtypeStruct(shape, jnp.float32),
        in_specs=[smem] * 4 + [vmem] + [anywhere] * 4 + [vmem, vmem],
        out_specs=pl.BlockSpec(memory_space=pltpu.HBM),
        scratch_shapes=[
            pltpu.VMEM(start.shape, jnp.float32),
            pltpu.VMEM((releases, levels, chunks, rows, LANES), jnp.float32),
            pltpu.VMEM((2, 4, levels, rows, width), jnp.bfloat16),
            pltpu.VMEM((2,) + start.shape[1:], jnp.float32),
            pltpu.VMEM((3, levels, chunks, 8, LANES), jnp.float32),
            pltpu.SemaphoreType.DMA((4 * PIECES,)),
            pltpu.SemaphoreType.DMA((chunks,)),
        ],
        compiler_params=pltpu.CompilerParams(vmem_limit_bytes=36 * 2**20),
        cost_estimate=pl.CostEstimate(flops=120 * math.prod(shape), bytes_accessed=12 * math.prod(shape), transcendentals=0),
    )(*scalars, cells, amounts, start, mine, other, mine_last, other_last, near, far)


def halos(first, last):
    count = lax.axis_size("slab")
    up = [(i, (i + 1) % count) for i in range(count - 1)]
    down = [(j, i) for i, j in up]
    return lax.ppermute(last, "slab", up), lax.ppermute(first, "slab", down)


def body(concentration, wind_store, sources, emission, snapshot_ids):
    rows, width = concentration.shape[2:]
    full = rows * lax.axis_size("slab")
    cells = jnp.stack([
        sources // (full * width),
        sources // width % full - lax.axis_index("slab") * rows,
        sources % width,
    ])
    return steps(concentration.shape, *broadcast(wind_store, snapshot_ids, concentration), cells, emission)


def solution(mesh):
    placed = (
        P("rel", None, "slab", None),
        P("rel", None, None, "slab", None),
        P("rel"),
        P("rel"),
        P(),
    )
    return jax.shard_map(
        body, mesh=mesh, in_specs=placed, out_specs=P("rel", None, "slab", None), check_vma=False
    )
```

```python
import functools
import math
import jax
import jax.numpy as jnp
from jax import lax
from jax.experimental import pallas as pl
from jax.experimental.pallas import tpu as pltpu
from jax.sharding import PartitionSpec as P

LANES = 128
PAD = 16


PIECES = 4
PIECE = (4, 2, 16, 1024)
LINKS = 3
PHASES = 4

SCHEDULES = (
    (
        (4, 5, 0, -1, -1, -1, -1, -1, -1, -1, -1, -1, -1, -1, -1, -1, -1, -1, -1, -1, -1, -1, -1, -1),
        (3, 1, 7, -1, 0, -1, 4, -1, 4, -1, -1, -1, -1, -1, -1, -1, -1, -1, -1, 5, 5, -1, -1, -1),
        (1, 2, 6, 7, -1, -1, -1, -1, 3, -1, -1, -1, -1, 5, 4, -1, -1, -1, -1, 1, 1, 5, 0, 0),
        (0, 6, 2, 6, 7, -1, 3, -1, 1, 3, 4, 7, 4, 4, 1, 4, 0, 0, -1, 2, 2, 1, 5, -1),
        (5, 7, 3, 2, -1, -1, 7, -1, 3, 6, 7, 6, 3, 2, 2, 3, 5, -1, -1, 6, 6, -1, 7, 2),
    ),
    (
        (-1, -1, -1, -1, -1, -1, -1, -1, -1, -1, -1, -1, -1, -1, -1, -1, -1, -1, -1, -1, -1, -1, -1, -1),
        (1, 3, 0, 6, 4, 4, -1, -1, -1, -1, -1, -1, -1, -1, -1, -1, -1, -1, -1, -1, -1, -1, -1, -1),
        (0, 2, 1, 5, 0, 7, 1, -1, 1, 6, -1, -1, -1, -1, -1, -1, -1, -1, -1, 3, 3, -1, 4, 4),
        (4, 7, 2, 7, 1, 5, 0, -1, 0, 5, -1, 5, 1, 3, 1, 6, 4, 4, -1, 2, 4, -1, 0, 0),
        (7, 5, 3, 2, 7, 6, 5, -1, 3, 7, -1, 6, 3, 2, 2, 5, 5, 6, -1, 7, 2, -1, 3, 6),
    ),
    (
        (-1, -1, -1, -1, -1, -1, -1, -1, -1, -1, -1, -1, -1, -1, -1, -1, -1, -1, -1, -1, -1, -1, -1, -1),
        (1, 0, 1, -1, -1, -1, 6, 5, 4, -1, -1, -1, -1, -1, -1, -1, -1, -1, -1, -1, -1, -1, -1, -1),
        (0, 3, 2, 1, 1, -1, 5, 4, 7, 4, 4, -1, 6, -1, 6, -1, -1, -1, -1, 0, 0, -1, -1, -1),
        (2, 4, 3, 2, 2, -1, 1, 7, 0, 7, 7, -1, 5, -1, 0, 4, 6, 4, -1, 3, 3, 0, 1, 1),
        (2, 7, 5, 3, 7, -1, 2, 7, 5, 2, 6, -1, 5, 3, 5, 6, -1, 7, 6, -1, 5, -1, 3, 2),
    ),
    (
        (-1, -1, -1, -1, -1, -1, -1, -1, -1, -1, -1, -1, -1, -1, -1, -1, -1, -1, -1, -1, -1, -1, -1, -1),
        (0, 1, 0, -1, -1, -1, -1, -1, -1, 4, 5, 6, -1, -1, -1, -1, -1, -1, -1, -1, -1, -1, -1, -1),
        (1, 2, 3, -1, 0, 5, 0, -1, 0, 7, 6, 4, -1, -1, -1, 4, -1, 4, -1, 1, 1, -1, -1, -1),
        (3, 5, 2, 3, 6, -1, 6, 4, 1, 5, 4, 7, 0, 1, 1, -1, -1, 7, 1, 2, 2, 1, 0, 4),
        (5, 3, 5, 2, 3, 6, 3, 7, 6, 3, 7, 7, 7, 2, 2, 7, -1, 7, -1, 5, 5, 2, 6, 6),
    ),
    (
        (-1, -1, -1, -1, -1, -1, -1, -1, -1, -1, -1, -1, -1, -1, -1, -1, -1, -1, -1, -1, -1, -1, -1, -1),
        (0, 0, 1, -1, -1, -1, -1, -1, -1, -1, -1, -1, 4, 6, 4, -1, -1, -1, -1, -1, -1, -1, -1, -1),
        (3, 1, 2, 1, 1, -1, -1, 6, 0, -1, -1, -1, 6, 7, 5, 4, 4, -1, -1, -1, 0, -1, -1, -1),
        (3, 2, 3, 2, 2, -1, 0, 7, 3, 1, 4, 1, 5, 4, 7, 5, 5, 5, 4, 1, 6, 0, 0, -1),
        (7, 3, 7, 3, 3, -1, 3, 6, 6, 3, 5, 2, 7, 5, 6, 7, 7, -1, 5, 2, 2, 6, 2, 6),
    ),
    (
        (-1, -1, -1, -1, -1, -1, -1, -1, -1, -1, -1, -1, -1, -1, -1, -1, -1, -1, -1, -1, -1, -1, -1, -1),
        (1, 2, 0, -1, -1, -1, -1, -1, -1, -1, -1, -1, -1, -1, -1, 6, 4, 7, -1, -1, -1, -1, -1, -1),
        (0, 3, 1, 0, 0, -1, 1, -1, 1, -1, 4, -1, -1, 7, -1, 5, 6, 4, 2, -1, 2, 6, -1, 6),
        (2, 1, 3, -1, 1, 4, 0, 7, -1, 1, 0, 6, 4, 4, 7, 4, 5, -1, -1, 3, 6, 5, 0, 0),
        (7, 7, 7, 3, 3, 5, 2, 2, 2, -1, -1, 5, 3, 3, 3, 7, 7, 5, 6, 6, 2, 2, 2, 5),
    ),
    (
        (-1, -1, -1, -1, -1, -1, -1, -1, -1, -1, -1, -1, -1, -1, -1, -1, -1, -1, -1, -1, -1, -1, -1, -1),
        (0, 0, 1, -1, -1, -1, -1, -1, -1, -1, -1, -1, -1, -1, -1, -1, -1, -1, 6, 7, 4, -1, -1, -1),
        (3, 1, 2, 1, 1, -1, 0, -1, 0, -1, -1, -1, -1, 7, 7, -1, -1, -1, 4, 5, 6, 4, 4, -1),
        (4, 2, 3, 2, 2, -1, -1, 7, 3, 1, 0, 1, -1, 5, 0, 7, 4, 4, 5, 1, 0, 6, 6, -1),
        (6, 3, 5, 6, 3, -1, 3, -1, 5, 3, -1, 2, -1, -1, 5, -1, 7, 6, -1, 2, 5, 7, 2, -1),
    ),
    (
        (-1, -1, -1, -1, -1, -1, -1, -1, -1, -1, -1, -1, -1, -1, -1, -1, -1, -1, -1, -1, -1, -1, -1, -1),
        (0, 1, 2, -1, -1, -1, -1, -1, -1, -1, -1, -1, -1, -1, -1, -1, -1, -1, -1, -1, -1, 4, 7, 4),
        (1, 3, 0, 4, -1, -1, 0, -1, 0, -1, -1, -1, -1, -1, -1, -1, 7, -1, -1, 4, 1, 5, 6, 5),
        (3, 2, 1, 2, 0, 5, 1, -1, 1, 4, 0, 7, 0, 4, 0, -1, 6, 7, 4, 5, 3, 5, 1, 6),
        (2, 2, 3, 5, 2, -1, 3, 7, 3, 2, 6, 6, 7, 5, 5, 7, -1, 6, 6, 2, 6, 7, 3, 5),
    ),
)


def parts_of(snap, piece, half, tile, held):
    if snap == 0:
        at = pl.multiple_of(half * 32 + 16 * ((piece // 2) ^ half), 16)
        return [(tile.at[:, pl.ds(2 * (piece % 2), 2), pl.ds(at, 16), :], held)]
    return [
        (tile.at[(piece + 3) % 4, :, pl.ds(pl.multiple_of(half * 32 + 16 * part, 16), 16), :], held.at[:, part])
        for part in range(2)
    ]


def plan(ids_ref, table_ref):
    chip = lax.axis_index("rel") >> 1
    first = ids_ref[0] >> 2
    second = ids_ref[1] >> 2

    def place(of):
        return 2 * (((of >> 1) - (first >> 1)) & 3) + ((of ^ first) & 1)

    here = place(chip)
    row = place(second) * 5
    z, h = here >> 1, here & 1
    sources = (2 * ((z - 1) & 3) + h, 2 * ((z + 1) & 3) + h, 2 * z + 1 - h)

    def sent(phase, link):
        return table_ref[(row + phase) * 24 + here * LINKS + link]

    def got(phase, link):
        return table_ref[(row + phase) * 24 + sources[link] * LINKS + link]

    return sent, got


def run_copies(copies, stages=(True, False)):
    for begin in stages:
        for condition, source, target, sem in copies:
            def act(source=source, target=target, sem=sem):
                copy = pltpu.make_async_copy(source, target, sem)
                if begin:
                    copy.start()
                else:
                    copy.wait()
            if condition is None:
                act()
            else:
                pl.when(condition)(act)


def run_staged(loads, stores):
    run_copies(loads)
    run_copies(stores)


def share_kernel(ids_ref, store_ref, out_ref, stage, sems):
    core = lax.axis_index("rel") & 1
    slots = range(2 * PIECES)
    loads = []
    for slot in slots:
        store = store_ref.at[ids_ref[slot // PIECES] & 1]
        for part, (source, target) in enumerate(parts_of(slot // PIECES, slot % PIECES, 1 - core, store, stage.at[slot])):
            loads.append((None, source, target, sems.at[2 * slot + part]))
    run_staged(loads, [(None, stage.at[slot], out_ref.at[slot], sems.at[slot]) for slot in slots])


def first_kernel(phase, brought, keeps, ids_ref, table_ref, store_ref, shared_ref, *rest):
    arrived, outs, held_ref = rest[:brought], rest[brought : brought + LINKS], rest[brought + LINKS]
    stage, sems = rest[-2:]
    me = lax.axis_index("rel")
    core = me & 1
    sent, got = plan(ids_ref, table_ref)
    loads, stores = [], []
    for slot in range(2 * PIECES):
        root = ids_ref[slot // PIECES] >> 1
        store = store_ref.at[ids_ref[slot // PIECES] & 1]
        for part, (source, target) in enumerate(parts_of(slot // PIECES, slot % PIECES, core, store, stage.at[slot])):
            loads.append((root == me, source, target, sems.at[2 * slot + part]))
        loads.append((root == (me ^ 1), shared_ref.at[slot], stage.at[slot], sems.at[2 * slot]))
        held = (root >> 1) == (me >> 1)
        for link in range(LINKS):
            chosen = jnp.logical_and(held, sent(phase, link) == slot)
            stores.append((chosen, stage.at[slot], outs[link], sems.at[link]))
        if keeps:
            stores.append((held, stage.at[slot], held_ref.at[slot], sems.at[2 * LINKS + slot]))
    for way in range(brought):
        slot = got(0, way)
        at = 2 * PIECES + way
        loads.append((None, arrived[way], stage.at[at], sems.at[4 * PIECES + way]))
        for link in range(LINKS):
            chosen = jnp.logical_and(slot >= 0, sent(phase, link) == slot)
            stores.append((chosen, stage.at[at], outs[link], sems.at[link]))
        stores.append((slot >= 0, stage.at[at], held_ref.at[jnp.maximum(slot, 0)], sems.at[LINKS + way]))
    run_staged(loads, stores)


def forward_kernel(phase, ids_ref, table_ref, *rest):
    arrived, held_ref, outs, stage, sems = rest[:LINKS], rest[LINKS], rest[LINKS + 1 : -2], rest[-2], rest[-1]
    sent, got = plan(ids_ref, table_ref)
    loads, stores = [], []
    for link in range(LINKS):
        slot = sent(phase + 1, link)
        loads.extend(
            (condition, source, stage.at[link], sems.at[link])
            for condition, source in wherever(slot, phase, got, arrived, held_ref)
        )
        stores.append((slot >= 0, stage.at[link], outs[link], sems.at[link]))
    run_staged(loads, stores)


def keep_kernel(phase, ids_ref, table_ref, *rest):
    arrived, held_ref, stage, sems = rest[:LINKS], *rest[LINKS + 1 :]
    _, got = plan(ids_ref, table_ref)
    ways = range(LINKS)
    run_staged(
        [(got(phase, way) >= 0, arrived[way], stage.at[way], sems.at[way]) for way in ways],
        [(got(phase, way) >= 0, stage.at[way], held_ref.at[jnp.maximum(got(phase, way), 0)], sems.at[way]) for way in ways],
    )


def wherever(slot, phase, got, arrived, held_ref):
    older = slot >= 0
    places = []
    for way in range(LINKS):
        places.append((jnp.logical_and(slot >= 0, got(phase, way) == slot), arrived[way]))
        older = jnp.logical_and(older, got(phase, way) != slot)
    return [*places, (older, held_ref.at[jnp.maximum(slot, 0)])]


def edge_kernel(held_ref, out_ref, stage, stage_kd, rows, sems):
    core = lax.axis_index("rel") & 1
    run_copies([
        (None, held_ref.at[0], stage.at[0], sems.at[0]),
        (None, held_ref.at[1], stage.at[1], sems.at[1]),
        (None, held_ref.at[PIECES, :, core], stage_kd, sems.at[2]),
    ])
    rows[:, 10:, :] = jnp.zeros_like(rows[:, 10:, :])
    for level in range(4):
        def ends(block, count):
            block = block.astype(jnp.float32)
            return jnp.where(core == 0, block[:count], block[16 - count :])

        for channel in range(3):
            rows[level, 2 * channel : 2 * channel + 2, :] = ends(stage[level // 2, channel, level % 2], 2)
        rows[level, 6:9, :] = ends(stage[level // 2, 3, level % 2], 3)
        rows[level, 9:10, :] = ends(stage_kd[level], 1)
    out_ref[...] = rows[...].astype(jnp.bfloat16)


def moved(kernel, scalars, inputs, outs, scratch, aliases=None, vmem_outs=0):
    smem = pl.BlockSpec(memory_space=pltpu.SMEM)
    anywhere = pl.BlockSpec(memory_space=pl.ANY)
    return pl.pallas_call(
        kernel,
        out_shape=tuple(jax.ShapeDtypeStruct(shape, jnp.bfloat16) for shape in outs),
        in_specs=[smem] * len(scalars) + [anywhere] * len(inputs),
        out_specs=(pl.BlockSpec(memory_space=pltpu.VMEM),) * vmem_outs + (anywhere,) * (len(outs) - vmem_outs),
        scratch_shapes=scratch,
        input_output_aliases=aliases or {},
        compiler_params=pltpu.CompilerParams(vmem_limit_bytes=12 * 2**20),
        cost_estimate=pl.CostEstimate(flops=0, bytes_accessed=2**21, transcendentals=0),
    )(*scalars, *inputs)


def exchange(sends):
    shifts = ((1, 0), (3, 0), (0, 1))
    arrived = []
    for send, (dz, dh) in zip(sends, shifts):
        pairs = []
        for z in range(4):
            for h in range(2):
                for core in range(2):
                    pairs.append((z * 4 + h * 2 + core, (z + dz) % 4 * 4 + (h ^ dh) * 2 + core))
        arrived.append(lax.ppermute(send, "rel", pairs))
    return arrived


def other_core(value):
    return lax.ppermute(value, "rel", [(i, i ^ 1) for i in range(16)])


def broadcast(wind_store, ids, field):
    table = jnp.asarray(SCHEDULES, jnp.int32).reshape(-1)
    every = (2 * PIECES,) + PIECE
    dma = pltpu.SemaphoreType.DMA
    sent = [PIECE] * LINKS

    def stage(slots):
        return pltpu.VMEM((slots,) + PIECE, jnp.bfloat16)

    (shared,) = moved(share_kernel, (ids,), [wind_store], [every], [stage(2 * PIECES), dma((4 * PIECES,))])
    shared = other_core(shared)

    def begin(phase, keeps, wind_store, shared, arrived):
        return moved(
            functools.partial(first_kernel, phase, len(arrived), keeps), (ids, table), [wind_store, shared, *arrived],
            sent + [every] * keeps, [stage(2 * PIECES + LINKS), dma((4 * PIECES + LINKS,))],
        )

    def one_chip(wind_store, shared):
        return begin(1, True, wind_store, shared, exchange(begin(0, False, wind_store, shared, [])))

    *sends, held = lax.cond(
        ids[0] >> 2 == ids[1] >> 2, one_chip, lambda store, shared: begin(1, True, store, shared, []), wind_store, shared
    )
    ends = (field[:, :, :4], field[:, :, -4:])
    for phase in range(1, PHASES + 1):
        if phase == 2:
            *ends, sends[0] = lax.optimization_barrier((*ends, sends[0]))
            west, east = halos(*ends)
        arrived = exchange(sends)
        if phase == 3:
            west, east, arrived[0] = lax.optimization_barrier((west, east, arrived[0]))
        if phase == PHASES:
            held, arrived[0] = lax.optimization_barrier((held, arrived[0]))
            (edges,) = moved(
                edge_kernel, (), [held], [(4, 16, 1024)],
                [stage(2), pltpu.VMEM((4, 16, 1024), jnp.bfloat16), pltpu.VMEM((4, 16, 1024), jnp.float32), dma((3,))],
                vmem_outs=1,
            )
        else:
            sends = moved(
                functools.partial(forward_kernel, phase), (ids, table), [*arrived, held], sent, [stage(LINKS), dma((LINKS,))]
            )
            *sends, held = lax.optimization_barrier((*sends, held))
        (held,) = moved(
            functools.partial(keep_kernel, phase), (ids, table), [*arrived, held], [every], [stage(LINKS), dma((LINKS,))],
            {2 + LINKS: 0},
        )
    other = other_core(held)
    ends = []
    for flip in range(2):
        pairs = []
        for slab in range(8):
            for rel in range(16):
                to = slab - 1 + 2 * (rel & 1)
                if 0 <= to < 8:
                    pairs.append((slab * 16 + rel, to * 16 + (rel ^ flip)))
        ends.append(lax.ppermute(edges, ("slab", "rel"), pairs))
    after, west, east, held = lax.optimization_barrier((field, west, east, held))
    return lay_out(after, west, east), held, other, *ends


def shifted_y(here, left, right, lane):
    south_one = pltpu.roll(jnp.where(lane == LANES - 1, left, here), 1, 1)
    south_two = pltpu.roll(jnp.where(lane >= LANES - 2, left, here), 2, 1)
    north_one = pltpu.roll(jnp.where(lane == 0, right, here), LANES - 1, 1)
    north_two = pltpu.roll(jnp.where(lane <= 1, right, here), LANES - 2, 1)
    return south_two, south_one, north_one, north_two


def upwind(courant):
    sixth = courant * (1.0 / 6.0)
    far = jnp.abs(sixth)
    near = far + far
    tilt = 4.0 * sixth
    return near + tilt, near - tilt, far


def roll_one(here, left, right, lane):
    south = pltpu.roll(jnp.where(lane == LANES - 1, left, here), 1, 1)
    north = pltpu.roll(jnp.where(lane == 0, right, here), LANES - 1, 1)
    return south, north


def weights(level, levels, cx, cy, cz, kd_here, kd_west, kd_east, kd_left, kd_right, lane):
    middle = kd_here[level]
    kd_south, kd_north = roll_one(middle, kd_left, kd_right, lane)
    west, east = middle + kd_west, middle + kd_east
    south, north = middle + kd_south, middle + kd_north
    below = middle + kd_here[max(level - 1, 0)]
    above = middle + kd_here[min(level + 1, levels - 1)]
    w1, e1, far_x = upwind(cx)
    s1, n1, far_y = upwind(cy)
    b1, a1, far_z = upwind(cz)
    loss = 3.0 * (far_x + far_y + far_z) + ((west + east) + (south + north) + (below + above))
    positive = jnp.maximum(cz * (1.0 / 6.0), 0.0)
    by_level = [None] * levels
    by_level[level] = 1.0 - loss
    for offset, weight in ((-2, -positive), (-1, b1 + below), (1, a1 + above), (2, positive - far_z)):
        at = min(max(level + offset, 0), levels - 1)
        by_level[at] = weight if by_level[at] is None else by_level[at] + weight
    return (cx > 0.0, far_x, w1 + west, e1 + east), (cy > 0.0, far_y, s1 + south, n1 + north), by_level


def weighted(along_x, along_y, by_level, level, x_cells, columns, left, right, lane):
    center = columns[level]
    y_cells = shifted_y(center, left, right, lane)
    total = by_level[level] * center
    for (forward, far, behind, ahead), cells in ((along_y, y_cells), (along_x, x_cells)):
        total = total + (behind * cells[1] + ahead * cells[2])
        total = total - far * jnp.where(forward, cells[0], cells[3])
    for other, weight in enumerate(by_level):
        if other != level and weight is not None:
            total = total + weight * columns[other]
    return total


def lay_out_kernel(field_hbm, west_ref, east_ref, out_ref, sems):
    chunks = out_ref.shape[2]
    rows = out_ref.shape[3] - 2 * PAD
    copies = []
    for j in range(chunks):
        span = pl.ds(j * LANES, LANES)
        copies.append((None, field_hbm.at[:, :, :, span], out_ref.at[:, :, j, pl.ds(PAD, rows), :], sems.at[j]))
        out_ref[:, :, j, PAD - 4 : PAD, :] = west_ref[:, :, :, span]
        out_ref[:, :, j, PAD + rows : PAD + rows + 4, :] = east_ref[:, :, :, span]
    run_copies(copies)


def lay_out(field, west, east):
    releases, levels, rows, width = field.shape
    chunks = width // LANES
    vmem = pl.BlockSpec(memory_space=pltpu.VMEM)
    return pl.pallas_call(
        lay_out_kernel,
        out_shape=jax.ShapeDtypeStruct((releases, levels, chunks, rows + 2 * PAD, LANES), jnp.float32),
        in_specs=[pl.BlockSpec(memory_space=pltpu.HBM), vmem, vmem],
        out_specs=vmem,
        scratch_shapes=[pltpu.SemaphoreType.DMA((chunks,))],
        compiler_params=pltpu.CompilerParams(vmem_limit_bytes=16 * 2**20),
        cost_estimate=pl.CostEstimate(flops=0, bytes_accessed=2**23, transcendentals=0),
    )(field, west, east)


def steps_kernel(cells_ref, amount_ref, first, mine_ref, other_ref, *rest):
    near_ref, far_ref, out_hbm, second, result, winds, half_kds, halo_wind, wind_sems, out_sems = rest
    releases, levels, chunks, padded_rows, _ = first.shape
    rows = padded_rows - 2 * PAD
    core = lax.rem(lax.axis_index("rel"), 2)
    slab = lax.axis_index("slab")

    def store(j):
        return pltpu.make_async_copy(
            result.at[:, :, j],
            out_hbm.at[:, :, :, pl.ds(pl.multiple_of(j * LANES, LANES), LANES)],
            out_sems.at[j],
        )

    wind_copies = []
    for slot in range(2 * PIECES):
        snap = slot // PIECES
        for number, (held, half) in enumerate(((mine_ref, core), (other_ref, 1 - core))):
            for part, (target, source) in enumerate(parts_of(snap, slot % PIECES, half, winds.at[snap], held.at[slot])):
                wind_copies.append((None, source, target, wind_sems.at[4 * slot + 2 * number + part]))
    run_copies(wind_copies, (True,))

    lane = lax.broadcasted_iota(jnp.int32, (8, LANES), 1)
    sublane = lax.broadcasted_iota(jnp.int32, (8, LANES), 0)
    lane_row = lax.broadcasted_iota(jnp.int32, (1, LANES), 1)

    def span_of(j):
        return pl.ds(pl.multiple_of(j * LANES, LANES), LANES)

    def halo_rows(j, carry):
        span = span_of(j)
        near = near_ref[:, :, span].astype(jnp.float32)
        far = far_ref[:, :, span].astype(jnp.float32)
        east = jnp.where(core == 0, near, far)
        west = jnp.where(core == 0, far, near)
        for channel in range(3):
            halo_wind[channel, :, j, 0:2, :] = east[:, 2 * channel : 2 * channel + 2]
            halo_wind[channel, :, j, 6:8, :] = west[:, 2 * channel : 2 * channel + 2]
        half_kds[0, :, j, PAD + rows : PAD + rows + 3, :] = 0.5 * east[:, 6:9]
        half_kds[0, :, j, PAD - 3 : PAD, :] = 0.5 * west[:, 6:9]
        half_kds[1, :, j, PAD + rows : PAD + rows + 1, :] = 0.5 * east[:, 9:10]
        half_kds[1, :, j, PAD - 1 : PAD, :] = 0.5 * west[:, 9:10]
        return carry

    lax.fori_loop(0, chunks, halo_rows, 0)
    run_copies(wind_copies, (False,))

    def spread_kd(j, carry):
        for snap in range(2):
            for level in range(levels):
                half_kds[snap, level, j, PAD : PAD + rows, :] = 0.5 * winds[snap, 3, level, :, span_of(j)].astype(jnp.float32)
        return carry

    lax.fori_loop(0, chunks, spread_kd, 0)

    def chunk(snap, source, target, pad, j):
        before = lax.rem(j + chunks - 1, chunks)
        after = lax.rem(j + 1, chunks)
        span = span_of(j)
        half_kd = half_kds.at[snap]

        for start in range(0, rows, 16):
            for level in range(levels):
                courant = [
                    winds[snap, channel, level, pl.ds(start, 16), span].astype(jnp.float32) for channel in range(3)
                ]
                for half in range(2):
                    at = PAD + start + 8 * half
                    here = pl.ds(at, 8)
                    cx, cy, cz = (value[8 * half : 8 * half + 8] for value in courant)
                    along_x, along_y, by_level = weights(
                        level, levels, cx, cy, cz,
                        [half_kd[other, j, here, :] for other in range(levels)],
                        half_kd[level, j, pl.ds(at - 1, 8), :], half_kd[level, j, pl.ds(at + 1, 8), :],
                        half_kd[level, before, here, :], half_kd[level, after, here, :], lane,
                    )
                    for release in range(releases):
                        target[release, level, j, pl.ds(at - PAD + pad, 8), :] = weighted(
                            along_x, along_y, by_level, level,
                            [source[release, level, j, pl.ds(at + shift, 8), :] for shift in (-2, -1, 1, 2)],
                            [source[release, other, j, here, :] for other in range(levels)],
                            source[release, level, before, here, :], source[release, level, after, here, :], lane,
                        )

    def halo_chunk(j):
        before = lax.rem(j + chunks - 1, chunks)
        after = lax.rem(j + 1, chunks)
        kept = jnp.logical_or(
            jnp.logical_and(sublane < 4, slab < lax.axis_size("slab") - 1), jnp.logical_and(sublane >= 4, slab > 0)
        )

        def around(ref, index, shift=0):
            east = ref[(*index, pl.ds(PAD + rows + shift, 8), slice(None))]
            west = ref[(*index, pl.ds(PAD - 8 + shift, 8), slice(None))]
            return jnp.where(sublane < 4, east, west)

        half_kd = half_kds.at[0]
        for level in range(levels):
            along_x, along_y, by_level = weights(
                level, levels, *(halo_wind[channel, level, j] for channel in range(3)),
                [around(half_kd, (other, j)) for other in range(levels)],
                around(half_kd, (level, j), -1), around(half_kd, (level, j), 1),
                around(half_kd, (level, before)), around(half_kd, (level, after)), lane,
            )
            for release in range(releases):
                value = weighted(
                    along_x, along_y, by_level, level,
                    [around(first, (release, level, j), shift) for shift in (-2, -1, 1, 2)],
                    [around(first, (release, other, j)) for other in range(levels)],
                    around(first, (release, level, before)), around(first, (release, level, after)), lane,
                )
                value = jnp.where(kept, value, 0.0)
                second[release, level, j, PAD + rows : PAD + rows + 4, :] = value[0:4]
                second[release, level, j, PAD - 4 : PAD, :] = value[4:8]

    def emit(ref, j, pad, reach):
        for release in range(releases):
            at_row = cells_ref[1, release]
            inside = jnp.logical_and(at_row >= -reach, at_row < rows + reach)
            amount = jnp.where(inside, amount_ref[release], 0.0)
            row = pad + jnp.clip(at_row, -reach, rows + reach - 1)
            spot = (release, cells_ref[0, release], j, pl.ds(row, 1), slice(None))
            ref[spot] = ref[spot] + jnp.where(j * LANES + lane_row == cells_ref[2, release], amount, 0.0)

    def first_step(j, carry):
        chunk(0, first, second, PAD, j)
        halo_chunk(j)
        emit(second, j, PAD, 2)
        return carry

    def second_step(j, carry):
        chunk(1, second, result, 0, j)
        emit(result, j, 0, 0)
        store(j).start()
        return carry

    lax.fori_loop(0, chunks, first_step, 0)
    lax.fori_loop(0, chunks, second_step, 0)
    for j in range(chunks):
        store(j).wait()


def steps(shape, start, mine, other, near, far, cells, amounts):
    releases, levels, rows, width = shape
    chunks = width // LANES
    vmem = pl.BlockSpec(memory_space=pltpu.VMEM)
    smem = pl.BlockSpec(memory_space=pltpu.SMEM)
    anywhere = pl.BlockSpec(memory_space=pl.ANY)
    return pl.pallas_call(
        steps_kernel,
        out_shape=jax.ShapeDtypeStruct(shape, jnp.float32),
        in_specs=[smem, smem, vmem, anywhere, anywhere, vmem, vmem],
        out_specs=pl.BlockSpec(memory_space=pltpu.HBM),
        scratch_shapes=[
            pltpu.VMEM(start.shape, jnp.float32),
            pltpu.VMEM((releases, levels, chunks, rows, LANES), jnp.float32),
            pltpu.VMEM((2, 4, levels, rows, width), jnp.bfloat16),
            pltpu.VMEM((2,) + start.shape[1:], jnp.float32),
            pltpu.VMEM((3, levels, chunks, 8, LANES), jnp.float32),
            pltpu.SemaphoreType.DMA((8 * PIECES,)),
            pltpu.SemaphoreType.DMA((chunks,)),
        ],
        compiler_params=pltpu.CompilerParams(vmem_limit_bytes=36 * 2**20),
        cost_estimate=pl.CostEstimate(flops=120 * math.prod(shape), bytes_accessed=12 * math.prod(shape), transcendentals=0),
    )(cells, amounts, start, mine, other, near, far)


def halos(first, last):
    count = lax.axis_size("slab")
    up = [(i, (i + 1) % count) for i in range(count - 1)]
    down = [(j, i) for i, j in up]
    return lax.ppermute(last, "slab", up), lax.ppermute(first, "slab", down)


def body(concentration, wind_store, sources, emission, snapshot_ids):
    rows, width = concentration.shape[2:]
    full = rows * lax.axis_size("slab")
    cells = jnp.stack([
        sources // (full * width),
        sources // width % full - lax.axis_index("slab") * rows,
        sources % width,
    ])
    return steps(concentration.shape, *broadcast(wind_store, snapshot_ids, concentration), cells, emission)


def solution(mesh):
    placed = (
        P("rel", None, "slab", None),
        P("rel", None, None, "slab", None),
        P("rel"),
        P("rel"),
        P(),
    )
    return jax.shard_map(
        body, mesh=mesh, in_specs=placed, out_specs=P("rel", None, "slab", None), check_vma=False
    )
```

```python
import functools
import math
import jax
import jax.numpy as jnp
from jax import lax
from jax.experimental import pallas as pl
from jax.experimental.pallas import tpu as pltpu
from jax.sharding import PartitionSpec as P

LANES = 128
PAD = 16


PIECES = 4
PIECE = (4, 2, 16, 1024)
LINKS = 3
PHASES = 4

SCHEDULES = (
    (
        (4, 5, 0, -1, -1, -1, -1, -1, -1, -1, -1, -1, -1, -1, -1, -1, -1, -1, -1, -1, -1, -1, -1, -1),
        (3, 1, 7, -1, 0, -1, 4, -1, 4, -1, -1, -1, -1, -1, -1, -1, -1, -1, -1, 5, 5, -1, -1, -1),
        (1, 2, 6, 7, -1, -1, -1, -1, 3, -1, -1, -1, -1, 5, 4, -1, -1, -1, -1, 1, 1, 5, 0, 0),
        (0, 6, 2, 6, 7, -1, 3, -1, 1, 3, 4, 7, 4, 4, 1, 4, 0, 0, -1, 2, 2, 1, 5, -1),
        (5, 7, 3, 2, -1, -1, 7, -1, 3, 6, 7, 6, 3, 2, 2, 3, 5, -1, -1, 6, 6, -1, 7, 2),
    ),
    (
        (-1, -1, -1, -1, -1, -1, -1, -1, -1, -1, -1, -1, -1, -1, -1, -1, -1, -1, -1, -1, -1, -1, -1, -1),
        (1, 3, 0, 6, 4, 4, -1, -1, -1, -1, -1, -1, -1, -1, -1, -1, -1, -1, -1, -1, -1, -1, -1, -1),
        (0, 2, 1, 5, 0, 7, 1, -1, 1, 6, -1, -1, -1, -1, -1, -1, -1, -1, -1, 3, 3, -1, 4, 4),
        (4, 7, 2, 7, 1, 5, 0, -1, 0, 5, -1, 5, 1, 3, 1, 6, 4, 4, -1, 2, 4, -1, 0, 0),
        (7, 5, 3, 2, 7, 6, 5, -1, 3, 7, -1, 6, 3, 2, 2, 5, 5, 6, -1, 7, 2, -1, 3, 6),
    ),
    (
        (-1, -1, -1, -1, -1, -1, -1, -1, -1, -1, -1, -1, -1, -1, -1, -1, -1, -1, -1, -1, -1, -1, -1, -1),
        (1, 0, 1, -1, -1, -1, 6, 5, 4, -1, -1, -1, -1, -1, -1, -1, -1, -1, -1, -1, -1, -1, -1, -1),
        (0, 3, 2, 1, 1, -1, 5, 4, 7, 4, 4, -1, 6, -1, 6, -1, -1, -1, -1, 0, 0, -1, -1, -1),
        (2, 4, 3, 2, 2, -1, 1, 7, 0, 7, 7, -1, 5, -1, 0, 4, 6, 4, -1, 3, 3, 0, 1, 1),
        (2, 7, 5, 3, 7, -1, 2, 7, 5, 2, 6, -1, 5, 3, 5, 6, -1, 7, 6, -1, 5, -1, 3, 2),
    ),
    (
        (-1, -1, -1, -1, -1, -1, -1, -1, -1, -1, -1, -1, -1, -1, -1, -1, -1, -1, -1, -1, -1, -1, -1, -1),
        (0, 1, 0, -1, -1, -1, -1, -1, -1, 4, 5, 6, -1, -1, -1, -1, -1, -1, -1, -1, -1, -1, -1, -1),
        (1, 2, 3, -1, 0, 5, 0, -1, 0, 7, 6, 4, -1, -1, -1, 4, -1, 4, -1, 1, 1, -1, -1, -1),
        (3, 5, 2, 3, 6, -1, 6, 4, 1, 5, 4, 7, 0, 1, 1, -1, -1, 7, 1, 2, 2, 1, 0, 4),
        (5, 3, 5, 2, 3, 6, 3, 7, 6, 3, 7, 7, 7, 2, 2, 7, -1, 7, -1, 5, 5, 2, 6, 6),
    ),
    (
        (-1, -1, -1, -1, -1, -1, -1, -1, -1, -1, -1, -1, -1, -1, -1, -1, -1, -1, -1, -1, -1, -1, -1, -1),
        (0, 0, 1, -1, -1, -1, -1, -1, -1, -1, -1, -1, 4, 6, 4, -1, -1, -1, -1, -1, -1, -1, -1, -1),
        (3, 1, 2, 1, 1, -1, -1, 6, 0, -1, -1, -1, 6, 7, 5, 4, 4, -1, -1, -1, 0, -1, -1, -1),
        (3, 2, 3, 2, 2, -1, 0, 7, 3, 1, 4, 1, 5, 4, 7, 5, 5, 5, 4, 1, 6, 0, 0, -1),
        (7, 3, 7, 3, 3, -1, 3, 6, 6, 3, 5, 2, 7, 5, 6, 7, 7, -1, 5, 2, 2, 6, 2, 6),
    ),
    (
        (-1, -1, -1, -1, -1, -1, -1, -1, -1, -1, -1, -1, -1, -1, -1, -1, -1, -1, -1, -1, -1, -1, -1, -1),
        (1, 2, 0, -1, -1, -1, -1, -1, -1, -1, -1, -1, -1, -1, -1, 6, 4, 7, -1, -1, -1, -1, -1, -1),
        (0, 3, 1, 0, 0, -1, 1, -1, 1, -1, 4, -1, -1, 7, -1, 5, 6, 4, 2, -1, 2, 6, -1, 6),
        (2, 1, 3, -1, 1, 4, 0, 7, -1, 1, 0, 6, 4, 4, 7, 4, 5, -1, -1, 3, 6, 5, 0, 0),
        (7, 7, 7, 3, 3, 5, 2, 2, 2, -1, -1, 5, 3, 3, 3, 7, 7, 5, 6, 6, 2, 2, 2, 5),
    ),
    (
        (-1, -1, -1, -1, -1, -1, -1, -1, -1, -1, -1, -1, -1, -1, -1, -1, -1, -1, -1, -1, -1, -1, -1, -1),
        (0, 0, 1, -1, -1, -1, -1, -1, -1, -1, -1, -1, -1, -1, -1, -1, -1, -1, 6, 7, 4, -1, -1, -1),
        (3, 1, 2, 1, 1, -1, 0, -1, 0, -1, -1, -1, -1, 7, 7, -1, -1, -1, 4, 5, 6, 4, 4, -1),
        (4, 2, 3, 2, 2, -1, -1, 7, 3, 1, 0, 1, -1, 5, 0, 7, 4, 4, 5, 1, 0, 6, 6, -1),
        (6, 3, 5, 6, 3, -1, 3, -1, 5, 3, -1, 2, -1, -1, 5, -1, 7, 6, -1, 2, 5, 7, 2, -1),
    ),
    (
        (-1, -1, -1, -1, -1, -1, -1, -1, -1, -1, -1, -1, -1, -1, -1, -1, -1, -1, -1, -1, -1, -1, -1, -1),
        (0, 1, 2, -1, -1, -1, -1, -1, -1, -1, -1, -1, -1, -1, -1, -1, -1, -1, -1, -1, -1, 4, 7, 4),
        (1, 3, 0, 4, -1, -1, 0, -1, 0, -1, -1, -1, -1, -1, -1, -1, 7, -1, -1, 4, 1, 5, 6, 5),
        (3, 2, 1, 2, 0, 5, 1, -1, 1, 4, 0, 7, 0, 4, 0, -1, 6, 7, 4, 5, 3, 5, 1, 6),
        (2, 2, 3, 5, 2, -1, 3, 7, 3, 2, 6, 6, 7, 5, 5, 7, -1, 6, 6, 2, 6, 7, 3, 5),
    ),
)


def parts_of(snap, piece, half, tile, held):
    if snap == 0:
        at = pl.multiple_of(half * 32 + 16 * ((piece // 2) ^ half), 16)
        return [(tile.at[:, pl.ds(2 * (piece % 2), 2), pl.ds(at, 16), :], held)]
    return [
        (tile.at[(piece + 3) % 4, :, pl.ds(pl.multiple_of(half * 32 + 16 * part, 16), 16), :], held.at[:, part])
        for part in range(2)
    ]


def plan(ids_ref, table_ref):
    chip = lax.axis_index("rel") >> 1
    first = ids_ref[0] >> 2
    second = ids_ref[1] >> 2

    def place(of):
        return 2 * (((of >> 1) - (first >> 1)) & 3) + ((of ^ first) & 1)

    here = place(chip)
    row = place(second) * 5
    z, h = here >> 1, here & 1
    sources = (2 * ((z - 1) & 3) + h, 2 * ((z + 1) & 3) + h, 2 * z + 1 - h)

    def sent(phase, link):
        return table_ref[(row + phase) * 24 + here * LINKS + link]

    def got(phase, link):
        return table_ref[(row + phase) * 24 + sources[link] * LINKS + link]

    return sent, got


def run_copies(copies, stages=(True, False)):
    for begin in stages:
        for condition, source, target, sem in copies:
            def act(source=source, target=target, sem=sem):
                copy = pltpu.make_async_copy(source, target, sem)
                if begin:
                    copy.start()
                else:
                    copy.wait()
            if condition is None:
                act()
            else:
                pl.when(condition)(act)


def run_staged(loads, stores):
    run_copies(loads)
    run_copies(stores)


def share_kernel(ids_ref, store_ref, out_ref, stage, sems):
    core = lax.axis_index("rel") & 1
    slots = range(2 * PIECES)
    loads = []
    for slot in slots:
        store = store_ref.at[ids_ref[slot // PIECES] & 1]
        for part, (source, target) in enumerate(parts_of(slot // PIECES, slot % PIECES, 1 - core, store, stage.at[slot])):
            loads.append((None, source, target, sems.at[2 * slot + part]))
    run_staged(loads, [(None, stage.at[slot], out_ref.at[slot], sems.at[slot]) for slot in slots])


def first_kernel(phase, brought, keeps, ids_ref, table_ref, store_ref, shared_ref, *rest):
    arrived, outs, held_ref = rest[:brought], rest[brought : brought + LINKS], rest[brought + LINKS]
    stage, sems = rest[-2:]
    me = lax.axis_index("rel")
    core = me & 1
    sent, got = plan(ids_ref, table_ref)
    loads, stores = [], []
    for slot in range(2 * PIECES):
        root = ids_ref[slot // PIECES] >> 1
        store = store_ref.at[ids_ref[slot // PIECES] & 1]
        for part, (source, target) in enumerate(parts_of(slot // PIECES, slot % PIECES, core, store, stage.at[slot])):
            loads.append((root == me, source, target, sems.at[2 * slot + part]))
        loads.append((root == (me ^ 1), shared_ref.at[slot], stage.at[slot], sems.at[2 * slot]))
        held = (root >> 1) == (me >> 1)
        for link in range(LINKS):
            chosen = jnp.logical_and(held, sent(phase, link) == slot)
            stores.append((chosen, stage.at[slot], outs[link], sems.at[link]))
        if keeps:
            stores.append((held, stage.at[slot], held_ref.at[slot], sems.at[2 * LINKS + slot]))
    for way in range(brought):
        slot = got(0, way)
        at = 2 * PIECES + way
        loads.append((None, arrived[way], stage.at[at], sems.at[4 * PIECES + way]))
        for link in range(LINKS):
            chosen = jnp.logical_and(slot >= 0, sent(phase, link) == slot)
            stores.append((chosen, stage.at[at], outs[link], sems.at[link]))
        stores.append((slot >= 0, stage.at[at], held_ref.at[jnp.maximum(slot, 0)], sems.at[LINKS + way]))
    run_staged(loads, stores)


def forward_kernel(phase, ids_ref, table_ref, *rest):
    arrived, older, outs, stage, sems = rest[:LINKS], rest[LINKS : 2 * LINKS], rest[2 * LINKS : -2], rest[-2], rest[-1]
    sent, got = plan(ids_ref, table_ref)
    loads, stores = [], []
    for link in range(LINKS):
        slot = sent(phase + 1, link)
        loads.extend(
            (condition, source, stage.at[link], sems.at[link])
            for condition, source in wherever(slot, phase, got, arrived, older[link])
        )
        stores.append((slot >= 0, stage.at[link], outs[link], sems.at[link]))
    run_staged(loads, stores)


def keep_kernel(phase, brought, lays, ids_ref, table_ref, *rest):
    arrived, held_in, held_ref, outs = rest[:brought], rest[brought], rest[brought + 1], rest[brought + 2 : -2]
    stage, sems = rest[-2:]
    sent, got = plan(ids_ref, table_ref)
    loads, stores = [], []
    for way in range(brought):
        slot = got(phase, way)
        loads.append((slot >= 0, arrived[way], stage.at[way], sems.at[way]))
        stores.append((slot >= 0, stage.at[way], held_ref.at[jnp.maximum(slot, 0)], sems.at[way]))
    for link in range(LINKS * lays):
        slot = sent(phase + 2, link)
        at = LINKS + link
        older = slot >= 0
        for way in range(LINKS):
            older = jnp.logical_and(older, got(phase + 1, way) != slot)
        before = older
        for way in range(brought):
            now = got(phase, way) == slot
            stores.append((jnp.logical_and(older, now), stage.at[way], outs[link], sems.at[at]))
            before = jnp.logical_and(before, jnp.logical_not(now))
        loads.append((before, held_in.at[jnp.maximum(slot, 0)], stage.at[at], sems.at[at]))
        stores.append((before, stage.at[at], outs[link], sems.at[at]))
    run_staged(loads, stores)


def wherever(slot, phase, got, arrived, older_ref):
    older = slot >= 0
    places = []
    for way in range(LINKS):
        places.append((jnp.logical_and(slot >= 0, got(phase, way) == slot), arrived[way]))
        older = jnp.logical_and(older, got(phase, way) != slot)
    return [*places, (older, older_ref)]


def edge_kernel(held_ref, out_ref, stage, stage_kd, rows, sems):
    core = lax.axis_index("rel") & 1
    run_copies([
        (None, held_ref.at[0], stage.at[0], sems.at[0]),
        (None, held_ref.at[1], stage.at[1], sems.at[1]),
        (None, held_ref.at[PIECES, :, core], stage_kd, sems.at[2]),
    ])
    rows[:, 10:, :] = jnp.zeros_like(rows[:, 10:, :])
    for level in range(4):
        def ends(block, count):
            block = block.astype(jnp.float32)
            return jnp.where(core == 0, block[:count], block[16 - count :])

        for channel in range(3):
            rows[level, 2 * channel : 2 * channel + 2, :] = ends(stage[level // 2, channel, level % 2], 2)
        rows[level, 6:9, :] = ends(stage[level // 2, 3, level % 2], 3)
        rows[level, 9:10, :] = ends(stage_kd[level], 1)
    out_ref[...] = rows[...].astype(jnp.bfloat16)


def moved(kernel, scalars, inputs, outs, scratch, aliases=None, vmem_outs=0):
    smem = pl.BlockSpec(memory_space=pltpu.SMEM)
    anywhere = pl.BlockSpec(memory_space=pl.ANY)
    return pl.pallas_call(
        kernel,
        out_shape=tuple(jax.ShapeDtypeStruct(shape, jnp.bfloat16) for shape in outs),
        in_specs=[smem] * len(scalars) + [anywhere] * len(inputs),
        out_specs=(pl.BlockSpec(memory_space=pltpu.VMEM),) * vmem_outs + (anywhere,) * (len(outs) - vmem_outs),
        scratch_shapes=scratch,
        input_output_aliases=aliases or {},
        compiler_params=pltpu.CompilerParams(vmem_limit_bytes=12 * 2**20),
        cost_estimate=pl.CostEstimate(flops=0, bytes_accessed=2**21, transcendentals=0),
    )(*scalars, *inputs)


def exchange(sends):
    shifts = ((1, 0), (3, 0), (0, 1))
    arrived = []
    for send, (dz, dh) in zip(sends, shifts):
        pairs = []
        for z in range(4):
            for h in range(2):
                for core in range(2):
                    pairs.append((z * 4 + h * 2 + core, (z + dz) % 4 * 4 + (h ^ dh) * 2 + core))
        arrived.append(lax.ppermute(send, "rel", pairs))
    return arrived


def other_core(value):
    return lax.ppermute(value, "rel", [(i, i ^ 1) for i in range(16)])


def swap_ends(edges):
    ends = []
    for flip in range(2):
        pairs = []
        for slab in range(8):
            for rel in range(16):
                to = slab - 1 + 2 * (rel & 1)
                if 0 <= to < 8:
                    pairs.append((slab * 16 + rel, to * 16 + (rel ^ flip)))
        ends.append(lax.ppermute(edges, ("slab", "rel"), pairs))
    return ends


def broadcast(wind_store, ids, field):
    table = jnp.asarray(SCHEDULES, jnp.int32).reshape(-1)
    every = (2 * PIECES,) + PIECE
    dma = pltpu.SemaphoreType.DMA
    sent = [PIECE] * LINKS

    def stage(slots):
        return pltpu.VMEM((slots,) + PIECE, jnp.bfloat16)

    (shared,) = moved(share_kernel, (ids,), [wind_store], [every], [stage(2 * PIECES), dma((4 * PIECES,))])
    shared = other_core(shared)

    def begin(phase, keeps, wind_store, shared, arrived):
        return moved(
            functools.partial(first_kernel, phase, len(arrived), keeps), (ids, table), [wind_store, shared, *arrived],
            sent + [every] * keeps, [stage(2 * PIECES + LINKS), dma((4 * PIECES + LINKS,))],
        )

    def one_chip(wind_store, shared):
        return begin(1, True, wind_store, shared, exchange(begin(0, False, wind_store, shared, [])))

    *sends, held = lax.cond(
        ids[0] >> 2 == ids[1] >> 2, one_chip, lambda store, shared: begin(1, True, store, shared, []), wind_store, shared
    )
    ends = (field[:, :, :4], field[:, :, -4:])
    def keep(phase, arrived, held, lays):
        held, *older = moved(
            functools.partial(keep_kernel, phase, len(arrived), lays), (ids, table), [*arrived, held], [every] + sent * lays,
            [stage(2 * LINKS), dma((2 * LINKS,))], {2 + len(arrived): 0},
        )
        return held, older

    came = []
    for phase in range(1, PHASES + 1):
        if phase == 2:
            *ends, held = lax.optimization_barrier((*ends, held))
            west, east = halos(*ends)
        *sends, held = lax.optimization_barrier((*sends, held))
        held, older = keep(phase - 1, came, held, phase < PHASES)
        arrived = exchange(sends)
        if phase == 3:
            west, east, arrived[0] = lax.optimization_barrier((west, east, arrived[0]))
        if phase < PHASES:
            sends = moved(
                functools.partial(forward_kernel, phase), (ids, table), [*arrived, *older], sent, [stage(LINKS), dma((LINKS,))]
            )
            came = arrived
    (edges,) = moved(
        edge_kernel, (), [held], [(4, 16, 1024)],
        [stage(2), pltpu.VMEM((4, 16, 1024), jnp.bfloat16), pltpu.VMEM((4, 16, 1024), jnp.float32), dma((3,))],
        vmem_outs=1,
    )
    ends = swap_ends(edges)
    *ends, arrived[1] = lax.optimization_barrier((*ends, arrived[1]))
    held, _ = keep(PHASES, arrived, held, False)
    after, west, east, held = lax.optimization_barrier((field, west, east, held))
    return lay_out(after, west, east), held, other_core(held), *ends


def shifted_y(here, left, right, lane):
    south_one = pltpu.roll(jnp.where(lane == LANES - 1, left, here), 1, 1)
    south_two = pltpu.roll(jnp.where(lane >= LANES - 2, left, here), 2, 1)
    north_one = pltpu.roll(jnp.where(lane == 0, right, here), LANES - 1, 1)
    north_two = pltpu.roll(jnp.where(lane <= 1, right, here), LANES - 2, 1)
    return south_two, south_one, north_one, north_two


def upwind(courant):
    sixth = courant * (1.0 / 6.0)
    far = jnp.abs(sixth)
    near = far + far
    tilt = 4.0 * sixth
    return near + tilt, near - tilt, far


def roll_one(here, left, right, lane):
    south = pltpu.roll(jnp.where(lane == LANES - 1, left, here), 1, 1)
    north = pltpu.roll(jnp.where(lane == 0, right, here), LANES - 1, 1)
    return south, north


def weights(level, levels, cx, cy, cz, kd_here, kd_west, kd_east, kd_left, kd_right, lane):
    middle = kd_here[level]
    kd_south, kd_north = roll_one(middle, kd_left, kd_right, lane)
    west, east = middle + kd_west, middle + kd_east
    south, north = middle + kd_south, middle + kd_north
    below = middle + kd_here[max(level - 1, 0)]
    above = middle + kd_here[min(level + 1, levels - 1)]
    w1, e1, far_x = upwind(cx)
    s1, n1, far_y = upwind(cy)
    b1, a1, far_z = upwind(cz)
    loss = 3.0 * (far_x + far_y + far_z) + ((west + east) + (south + north) + (below + above))
    positive = jnp.maximum(cz * (1.0 / 6.0), 0.0)
    by_level = [None] * levels
    by_level[level] = 1.0 - loss
    for offset, weight in ((-2, -positive), (-1, b1 + below), (1, a1 + above), (2, positive - far_z)):
        at = min(max(level + offset, 0), levels - 1)
        by_level[at] = weight if by_level[at] is None else by_level[at] + weight
    return (cx > 0.0, far_x, w1 + west, e1 + east), (cy > 0.0, far_y, s1 + south, n1 + north), by_level


def weighted(along_x, along_y, by_level, level, x_cells, columns, left, right, lane):
    center = columns[level]
    y_cells = shifted_y(center, left, right, lane)
    total = by_level[level] * center
    for (forward, far, behind, ahead), cells in ((along_y, y_cells), (along_x, x_cells)):
        total = total + (behind * cells[1] + ahead * cells[2])
        total = total - far * jnp.where(forward, cells[0], cells[3])
    for other, weight in enumerate(by_level):
        if other != level and weight is not None:
            total = total + weight * columns[other]
    return total


def lay_out_kernel(field_hbm, west_ref, east_ref, out_ref, sems):
    chunks = out_ref.shape[2]
    rows = out_ref.shape[3] - 2 * PAD
    copies = []
    for j in range(chunks):
        span = pl.ds(j * LANES, LANES)
        copies.append((None, field_hbm.at[:, :, :, span], out_ref.at[:, :, j, pl.ds(PAD, rows), :], sems.at[j]))
        out_ref[:, :, j, PAD - 4 : PAD, :] = west_ref[:, :, :, span]
        out_ref[:, :, j, PAD + rows : PAD + rows + 4, :] = east_ref[:, :, :, span]
    run_copies(copies)


def lay_out(field, west, east):
    releases, levels, rows, width = field.shape
    chunks = width // LANES
    vmem = pl.BlockSpec(memory_space=pltpu.VMEM)
    return pl.pallas_call(
        lay_out_kernel,
        out_shape=jax.ShapeDtypeStruct((releases, levels, chunks, rows + 2 * PAD, LANES), jnp.float32),
        in_specs=[pl.BlockSpec(memory_space=pltpu.HBM), vmem, vmem],
        out_specs=vmem,
        scratch_shapes=[pltpu.SemaphoreType.DMA((chunks,))],
        compiler_params=pltpu.CompilerParams(vmem_limit_bytes=16 * 2**20),
        cost_estimate=pl.CostEstimate(flops=0, bytes_accessed=2**23, transcendentals=0),
    )(field, west, east)


def steps_kernel(cells_ref, amount_ref, first, mine_ref, other_ref, *rest):
    near_ref, far_ref, out_hbm, second, result, winds, half_kds, halo_wind, wind_sems, out_sems = rest
    releases, levels, chunks, padded_rows, _ = first.shape
    rows = padded_rows - 2 * PAD
    core = lax.rem(lax.axis_index("rel"), 2)
    slab = lax.axis_index("slab")

    def store(j):
        return pltpu.make_async_copy(
            result.at[:, :, j],
            out_hbm.at[:, :, :, pl.ds(pl.multiple_of(j * LANES, LANES), LANES)],
            out_sems.at[j],
        )

    wind_copies = []
    for slot in range(2 * PIECES):
        snap = slot // PIECES
        for number, (held, half) in enumerate(((mine_ref, core), (other_ref, 1 - core))):
            for part, (target, source) in enumerate(parts_of(snap, slot % PIECES, half, winds.at[snap], held.at[slot])):
                wind_copies.append((None, source, target, wind_sems.at[4 * slot + 2 * number + part]))
    run_copies(wind_copies, (True,))

    lane = lax.broadcasted_iota(jnp.int32, (8, LANES), 1)
    sublane = lax.broadcasted_iota(jnp.int32, (8, LANES), 0)
    lane_row = lax.broadcasted_iota(jnp.int32, (1, LANES), 1)

    def span_of(j):
        return pl.ds(pl.multiple_of(j * LANES, LANES), LANES)

    def halo_rows(j, carry):
        span = span_of(j)
        near = near_ref[:, :, span].astype(jnp.float32)
        far = far_ref[:, :, span].astype(jnp.float32)
        east = jnp.where(core == 0, near, far)
        west = jnp.where(core == 0, far, near)
        for channel in range(3):
            halo_wind[channel, :, j, 0:2, :] = east[:, 2 * channel : 2 * channel + 2]
            halo_wind[channel, :, j, 6:8, :] = west[:, 2 * channel : 2 * channel + 2]
        half_kds[0, :, j, PAD + rows : PAD + rows + 3, :] = 0.5 * east[:, 6:9]
        half_kds[0, :, j, PAD - 3 : PAD, :] = 0.5 * west[:, 6:9]
        half_kds[1, :, j, PAD + rows : PAD + rows + 1, :] = 0.5 * east[:, 9:10]
        half_kds[1, :, j, PAD - 1 : PAD, :] = 0.5 * west[:, 9:10]
        return carry

    lax.fori_loop(0, chunks, halo_rows, 0)
    run_copies(wind_copies, (False,))

    def spread_kd(j, carry):
        for snap in range(2):
            for level in range(levels):
                half_kds[snap, level, j, PAD : PAD + rows, :] = 0.5 * winds[snap, 3, level, :, span_of(j)].astype(jnp.float32)
        return carry

    lax.fori_loop(0, chunks, spread_kd, 0)

    def chunk(snap, source, target, pad, j):
        before = lax.rem(j + chunks - 1, chunks)
        after = lax.rem(j + 1, chunks)
        span = span_of(j)
        half_kd = half_kds.at[snap]

        for start in range(0, rows, 16):
            for level in range(levels):
                courant = [
                    winds[snap, channel, level, pl.ds(start, 16), span].astype(jnp.float32) for channel in range(3)
                ]
                for half in range(2):
                    at = PAD + start + 8 * half
                    here = pl.ds(at, 8)
                    cx, cy, cz = (value[8 * half : 8 * half + 8] for value in courant)
                    along_x, along_y, by_level = weights(
                        level, levels, cx, cy, cz,
                        [half_kd[other, j, here, :] for other in range(levels)],
                        half_kd[level, j, pl.ds(at - 1, 8), :], half_kd[level, j, pl.ds(at + 1, 8), :],
                        half_kd[level, before, here, :], half_kd[level, after, here, :], lane,
                    )
                    for release in range(releases):
                        target[release, level, j, pl.ds(at - PAD + pad, 8), :] = weighted(
                            along_x, along_y, by_level, level,
                            [source[release, level, j, pl.ds(at + shift, 8), :] for shift in (-2, -1, 1, 2)],
                            [source[release, other, j, here, :] for other in range(levels)],
                            source[release, level, before, here, :], source[release, level, after, here, :], lane,
                        )

    def halo_chunk(j):
        before = lax.rem(j + chunks - 1, chunks)
        after = lax.rem(j + 1, chunks)
        kept = jnp.logical_or(
            jnp.logical_and(sublane < 4, slab < lax.axis_size("slab") - 1), jnp.logical_and(sublane >= 4, slab > 0)
        )

        def around(ref, index, shift=0):
            east = ref[(*index, pl.ds(PAD + rows + shift, 8), slice(None))]
            west = ref[(*index, pl.ds(PAD - 8 + shift, 8), slice(None))]
            return jnp.where(sublane < 4, east, west)

        half_kd = half_kds.at[0]
        for level in range(levels):
            along_x, along_y, by_level = weights(
                level, levels, *(halo_wind[channel, level, j] for channel in range(3)),
                [around(half_kd, (other, j)) for other in range(levels)],
                around(half_kd, (level, j), -1), around(half_kd, (level, j), 1),
                around(half_kd, (level, before)), around(half_kd, (level, after)), lane,
            )
            for release in range(releases):
                value = weighted(
                    along_x, along_y, by_level, level,
                    [around(first, (release, level, j), shift) for shift in (-2, -1, 1, 2)],
                    [around(first, (release, other, j)) for other in range(levels)],
                    around(first, (release, level, before)), around(first, (release, level, after)), lane,
                )
                value = jnp.where(kept, value, 0.0)
                second[release, level, j, PAD + rows : PAD + rows + 4, :] = value[0:4]
                second[release, level, j, PAD - 4 : PAD, :] = value[4:8]

    def emit(ref, j, pad, reach):
        for release in range(releases):
            at_row = cells_ref[1, release]
            inside = jnp.logical_and(at_row >= -reach, at_row < rows + reach)
            amount = jnp.where(inside, amount_ref[release], 0.0)
            row = pad + jnp.clip(at_row, -reach, rows + reach - 1)
            spot = (release, cells_ref[0, release], j, pl.ds(row, 1), slice(None))
            ref[spot] = ref[spot] + jnp.where(j * LANES + lane_row == cells_ref[2, release], amount, 0.0)

    def first_step(j, carry):
        chunk(0, first, second, PAD, j)
        halo_chunk(j)
        emit(second, j, PAD, 2)
        return carry

    def second_step(j, carry):
        chunk(1, second, result, 0, j)
        emit(result, j, 0, 0)
        store(j).start()
        return carry

    lax.fori_loop(0, chunks, first_step, 0)
    lax.fori_loop(0, chunks, second_step, 0)
    for j in range(chunks):
        store(j).wait()


def steps(shape, start, mine, other, near, far, cells, amounts):
    releases, levels, rows, width = shape
    chunks = width // LANES
    vmem = pl.BlockSpec(memory_space=pltpu.VMEM)
    smem = pl.BlockSpec(memory_space=pltpu.SMEM)
    anywhere = pl.BlockSpec(memory_space=pl.ANY)
    return pl.pallas_call(
        steps_kernel,
        out_shape=jax.ShapeDtypeStruct(shape, jnp.float32),
        in_specs=[smem, smem, vmem, anywhere, anywhere, vmem, vmem],
        out_specs=pl.BlockSpec(memory_space=pltpu.HBM),
        scratch_shapes=[
            pltpu.VMEM(start.shape, jnp.float32),
            pltpu.VMEM((releases, levels, chunks, rows, LANES), jnp.float32),
            pltpu.VMEM((2, 4, levels, rows, width), jnp.bfloat16),
            pltpu.VMEM((2,) + start.shape[1:], jnp.float32),
            pltpu.VMEM((3, levels, chunks, 8, LANES), jnp.float32),
            pltpu.SemaphoreType.DMA((8 * PIECES,)),
            pltpu.SemaphoreType.DMA((chunks,)),
        ],
        compiler_params=pltpu.CompilerParams(vmem_limit_bytes=36 * 2**20),
        cost_estimate=pl.CostEstimate(flops=120 * math.prod(shape), bytes_accessed=12 * math.prod(shape), transcendentals=0),
    )(cells, amounts, start, mine, other, near, far)


def halos(first, last):
    count = lax.axis_size("slab")
    up = [(i, (i + 1) % count) for i in range(count - 1)]
    down = [(j, i) for i, j in up]
    return lax.ppermute(last, "slab", up), lax.ppermute(first, "slab", down)


def body(concentration, wind_store, sources, emission, snapshot_ids):
    rows, width = concentration.shape[2:]
    full = rows * lax.axis_size("slab")
    cells = jnp.stack([
        sources // (full * width),
        sources // width % full - lax.axis_index("slab") * rows,
        sources % width,
    ])
    return steps(concentration.shape, *broadcast(wind_store, snapshot_ids, concentration), cells, emission)


def solution(mesh):
    placed = (
        P("rel", None, "slab", None),
        P("rel", None, None, "slab", None),
        P("rel"),
        P("rel"),
        P(),
    )
    return jax.shard_map(
        body, mesh=mesh, in_specs=placed, out_specs=P("rel", None, "slab", None), check_vma=False
    )
```

```python
import functools
import math
import jax
import jax.numpy as jnp
from jax import lax
from jax.experimental import pallas as pl
from jax.experimental.pallas import tpu as pltpu
from jax.sharding import PartitionSpec as P

LANES = 128
PAD = 16


PIECES = 4
PIECE = (4, 2, 16, 1024)
LINKS = 3
PHASES = 4

SCHEDULES = (
    (
        (4, 5, 0, -1, -1, -1, -1, -1, -1, -1, -1, -1, -1, -1, -1, -1, -1, -1, -1, -1, -1, -1, -1, -1),
        (3, 1, 7, -1, 0, -1, 4, -1, 4, -1, -1, -1, -1, -1, -1, -1, -1, -1, -1, 5, 5, -1, -1, -1),
        (1, 2, 6, 7, -1, -1, -1, -1, 3, -1, -1, -1, -1, 5, 4, -1, -1, -1, -1, 1, 1, 5, 0, 0),
        (0, 6, 2, 6, 7, -1, 3, -1, 1, 3, 4, 7, 4, 4, 1, 4, 0, 0, -1, 2, 2, 1, 5, -1),
        (5, 7, 3, 2, -1, -1, 7, -1, 3, 6, 7, 6, 3, 2, 2, 3, 5, -1, -1, 6, 6, -1, 7, 2),
    ),
    (
        (-1, -1, -1, -1, -1, -1, -1, -1, -1, -1, -1, -1, -1, -1, -1, -1, -1, -1, -1, -1, -1, -1, -1, -1),
        (1, 3, 0, 6, 4, 4, -1, -1, -1, -1, -1, -1, -1, -1, -1, -1, -1, -1, -1, -1, -1, -1, -1, -1),
        (0, 2, 1, 5, 0, 7, 1, -1, 1, 6, -1, -1, -1, -1, -1, -1, -1, -1, -1, 3, 3, -1, 4, 4),
        (4, 7, 2, 7, 1, 5, 0, -1, 0, 5, -1, 5, 1, 3, 1, 6, 4, 4, -1, 2, 4, -1, 0, 0),
        (7, 5, 3, 2, 7, 6, 5, -1, 3, 7, -1, 6, 3, 2, 2, 5, 5, 6, -1, 7, 2, -1, 3, 6),
    ),
    (
        (-1, -1, -1, -1, -1, -1, -1, -1, -1, -1, -1, -1, -1, -1, -1, -1, -1, -1, -1, -1, -1, -1, -1, -1),
        (1, 0, 1, -1, -1, -1, 6, 5, 4, -1, -1, -1, -1, -1, -1, -1, -1, -1, -1, -1, -1, -1, -1, -1),
        (0, 3, 2, 1, 1, -1, 5, 4, 7, 4, 4, -1, 6, -1, 6, -1, -1, -1, -1, 0, 0, -1, -1, -1),
        (2, 4, 3, 2, 2, -1, 1, 7, 0, 7, 7, -1, 5, -1, 0, 4, 6, 4, -1, 3, 3, 0, 1, 1),
        (2, 7, 5, 3, 7, -1, 2, 7, 5, 2, 6, -1, 5, 3, 5, 6, -1, 7, 6, -1, 5, -1, 3, 2),
    ),
    (
        (-1, -1, -1, -1, -1, -1, -1, -1, -1, -1, -1, -1, -1, -1, -1, -1, -1, -1, -1, -1, -1, -1, -1, -1),
        (0, 1, 0, -1, -1, -1, -1, -1, -1, 4, 5, 6, -1, -1, -1, -1, -1, -1, -1, -1, -1, -1, -1, -1),
        (1, 2, 3, -1, 0, 5, 0, -1, 0, 7, 6, 4, -1, -1, -1, 4, -1, 4, -1, 1, 1, -1, -1, -1),
        (3, 5, 2, 3, 6, -1, 6, 4, 1, 5, 4, 7, 0, 1, 1, -1, -1, 7, 1, 2, 2, 1, 0, 4),
        (5, 3, 5, 2, 3, 6, 3, 7, 6, 3, 7, 7, 7, 2, 2, 7, -1, 7, -1, 5, 5, 2, 6, 6),
    ),
    (
        (-1, -1, -1, -1, -1, -1, -1, -1, -1, -1, -1, -1, -1, -1, -1, -1, -1, -1, -1, -1, -1, -1, -1, -1),
        (0, 0, 1, -1, -1, -1, -1, -1, -1, -1, -1, -1, 4, 6, 4, -1, -1, -1, -1, -1, -1, -1, -1, -1),
        (3, 1, 2, 1, 1, -1, -1, 6, 0, -1, -1, -1, 6, 7, 5, 4, 4, -1, -1, -1, 0, -1, -1, -1),
        (3, 2, 3, 2, 2, -1, 0, 7, 3, 1, 4, 1, 5, 4, 7, 5, 5, 5, 4, 1, 6, 0, 0, -1),
        (7, 3, 7, 3, 3, -1, 3, 6, 6, 3, 5, 2, 7, 5, 6, 7, 7, -1, 5, 2, 2, 6, 2, 6),
    ),
    (
        (-1, -1, -1, -1, -1, -1, -1, -1, -1, -1, -1, -1, -1, -1, -1, -1, -1, -1, -1, -1, -1, -1, -1, -1),
        (1, 2, 0, -1, -1, -1, -1, -1, -1, -1, -1, -1, -1, -1, -1, 6, 4, 7, -1, -1, -1, -1, -1, -1),
        (0, 3, 1, 0, 0, -1, 1, -1, 1, -1, 4, -1, -1, 7, -1, 5, 6, 4, 2, -1, 2, 6, -1, 6),
        (2, 1, 3, -1, 1, 4, 0, 7, -1, 1, 0, 6, 4, 4, 7, 4, 5, -1, -1, 3, 6, 5, 0, 0),
        (7, 7, 7, 3, 3, 5, 2, 2, 2, -1, -1, 5, 3, 3, 3, 7, 7, 5, 6, 6, 2, 2, 2, 5),
    ),
    (
        (-1, -1, -1, -1, -1, -1, -1, -1, -1, -1, -1, -1, -1, -1, -1, -1, -1, -1, -1, -1, -1, -1, -1, -1),
        (0, 0, 1, -1, -1, -1, -1, -1, -1, -1, -1, -1, -1, -1, -1, -1, -1, -1, 6, 7, 4, -1, -1, -1),
        (3, 1, 2, 1, 1, -1, 0, -1, 0, -1, -1, -1, -1, 7, 7, -1, -1, -1, 4, 5, 6, 4, 4, -1),
        (4, 2, 3, 2, 2, -1, -1, 7, 3, 1, 0, 1, -1, 5, 0, 7, 4, 4, 5, 1, 0, 6, 6, -1),
        (6, 3, 5, 6, 3, -1, 3, -1, 5, 3, -1, 2, -1, -1, 5, -1, 7, 6, -1, 2, 5, 7, 2, -1),
    ),
    (
        (-1, -1, -1, -1, -1, -1, -1, -1, -1, -1, -1, -1, -1, -1, -1, -1, -1, -1, -1, -1, -1, -1, -1, -1),
        (0, 1, 2, -1, -1, -1, -1, -1, -1, -1, -1, -1, -1, -1, -1, -1, -1, -1, -1, -1, -1, 4, 7, 4),
        (1, 3, 0, 4, -1, -1, 0, -1, 0, -1, -1, -1, -1, -1, -1, -1, 7, -1, -1, 4, 1, 5, 6, 5),
        (3, 2, 1, 2, 0, 5, 1, -1, 1, 4, 0, 7, 0, 4, 0, -1, 6, 7, 4, 5, 3, 5, 1, 6),
        (2, 2, 3, 5, 2, -1, 3, 7, 3, 2, 6, 6, 7, 5, 5, 7, -1, 6, 6, 2, 6, 7, 3, 5),
    ),
)


def parts_of(snap, piece, half, tile, held):
    if snap == 0:
        at = pl.multiple_of(half * 32 + 16 * ((piece // 2) ^ half), 16)
        return [(tile.at[:, pl.ds(2 * (piece % 2), 2), pl.ds(at, 16), :], held)]
    return [
        (tile.at[(piece + 3) % 4, :, pl.ds(pl.multiple_of(half * 32 + 16 * part, 16), 16), :], held.at[:, part])
        for part in range(2)
    ]


def plan(ids_ref, table_ref):
    chip = lax.axis_index("rel") >> 1
    first = ids_ref[0] >> 2
    second = ids_ref[1] >> 2

    def place(of):
        return 2 * (((of >> 1) - (first >> 1)) & 3) + ((of ^ first) & 1)

    here = place(chip)
    row = place(second) * 5
    z, h = here >> 1, here & 1
    sources = (2 * ((z - 1) & 3) + h, 2 * ((z + 1) & 3) + h, 2 * z + 1 - h)

    def sent(phase, link):
        return table_ref[(row + phase) * 24 + here * LINKS + link]

    def got(phase, link):
        return table_ref[(row + phase) * 24 + sources[link] * LINKS + link]

    return sent, got


def run_copies(copies, stages=(True, False)):
    for begin in stages:
        for condition, source, target, sem in copies:
            def act(source=source, target=target, sem=sem):
                copy = pltpu.make_async_copy(source, target, sem)
                if begin:
                    copy.start()
                else:
                    copy.wait()
            if condition is None:
                act()
            else:
                pl.when(condition)(act)


def run_staged(loads, stores):
    run_copies(loads)
    run_copies(stores)


def share_kernel(ids_ref, store_ref, out_ref, stage, sems):
    core = lax.axis_index("rel") & 1
    slots = range(2 * PIECES)
    loads = []
    for slot in slots:
        store = store_ref.at[ids_ref[slot // PIECES] & 1]
        for part, (source, target) in enumerate(parts_of(slot // PIECES, slot % PIECES, 1 - core, store, stage.at[slot])):
            loads.append((None, source, target, sems.at[2 * slot + part]))
    run_staged(loads, [(None, stage.at[slot], out_ref.at[slot], sems.at[slot]) for slot in slots])


def first_kernel(phase, brought, keeps, ids_ref, table_ref, store_ref, shared_ref, *rest):
    arrived, outs, held_ref = rest[:brought], rest[brought : brought + LINKS], rest[brought + LINKS]
    stage, sems = rest[-2:]
    me = lax.axis_index("rel")
    core = me & 1
    sent, got = plan(ids_ref, table_ref)
    loads, stores = [], []
    for slot in range(2 * PIECES):
        root = ids_ref[slot // PIECES] >> 1
        store = store_ref.at[ids_ref[slot // PIECES] & 1]
        for part, (source, target) in enumerate(parts_of(slot // PIECES, slot % PIECES, core, store, stage.at[slot])):
            loads.append((root == me, source, target, sems.at[2 * slot + part]))
        loads.append((root == (me ^ 1), shared_ref.at[slot], stage.at[slot], sems.at[2 * slot]))
        held = (root >> 1) == (me >> 1)
        for link in range(LINKS):
            chosen = jnp.logical_and(held, sent(phase, link) == slot)
            stores.append((chosen, stage.at[slot], outs[link], sems.at[link]))
        if keeps:
            stores.append((held, stage.at[slot], held_ref.at[slot], sems.at[2 * LINKS + slot]))
    for way in range(brought):
        slot = got(0, way)
        at = 2 * PIECES + way
        loads.append((None, arrived[way], stage.at[at], sems.at[4 * PIECES + way]))
        for link in range(LINKS):
            chosen = jnp.logical_and(slot >= 0, sent(phase, link) == slot)
            stores.append((chosen, stage.at[at], outs[link], sems.at[link]))
        stores.append((slot >= 0, stage.at[at], held_ref.at[jnp.maximum(slot, 0)], sems.at[LINKS + way]))
    run_staged(loads, stores)


def forward_kernel(phase, ids_ref, table_ref, *rest):
    arrived, older, outs, stage, sems = rest[:LINKS], rest[LINKS : 2 * LINKS], rest[2 * LINKS : -2], rest[-2], rest[-1]
    sent, got = plan(ids_ref, table_ref)
    loads, stores = [], []
    for link in range(LINKS):
        slot = sent(phase + 1, link)
        loads.extend(
            (condition, source, stage.at[link], sems.at[link])
            for condition, source in wherever(slot, phase, got, arrived, older[link])
        )
        stores.append((slot >= 0, stage.at[link], outs[link], sems.at[link]))
    run_staged(loads, stores)


def keep_kernel(phase, brought, lays, ids_ref, table_ref, *rest):
    arrived, held_in, held_ref, outs = rest[:brought], rest[brought], rest[brought + 1], rest[brought + 2 : -2]
    stage, sems = rest[-2:]
    sent, got = plan(ids_ref, table_ref)
    loads, stores = [], []
    for way in range(brought):
        slot = got(phase, way)
        loads.append((slot >= 0, arrived[way], stage.at[way], sems.at[way]))
        stores.append((slot >= 0, stage.at[way], held_ref.at[jnp.maximum(slot, 0)], sems.at[way]))
    for link in range(LINKS * lays):
        slot = sent(phase + 2, link)
        at = LINKS + link
        older = slot >= 0
        for way in range(LINKS):
            older = jnp.logical_and(older, got(phase + 1, way) != slot)
        before = older
        for way in range(brought):
            now = got(phase, way) == slot
            stores.append((jnp.logical_and(older, now), stage.at[way], outs[link], sems.at[at]))
            before = jnp.logical_and(before, jnp.logical_not(now))
        loads.append((before, held_in.at[jnp.maximum(slot, 0)], stage.at[at], sems.at[at]))
        stores.append((before, stage.at[at], outs[link], sems.at[at]))
    run_staged(loads, stores)


def wherever(slot, phase, got, arrived, older_ref):
    older = slot >= 0
    places = []
    for way in range(LINKS):
        places.append((jnp.logical_and(slot >= 0, got(phase, way) == slot), arrived[way]))
        older = jnp.logical_and(older, got(phase, way) != slot)
    return [*places, (older, older_ref)]


def edge_kernel(held_ref, out_ref, stage, stage_kd, rows, sems):
    core = lax.axis_index("rel") & 1
    run_copies([
        (None, held_ref.at[0], stage.at[0], sems.at[0]),
        (None, held_ref.at[1], stage.at[1], sems.at[1]),
        (None, held_ref.at[PIECES, :, core], stage_kd, sems.at[2]),
    ])
    rows[:, 10:, :] = jnp.zeros_like(rows[:, 10:, :])
    for level in range(4):
        def ends(block, count):
            block = block.astype(jnp.float32)
            return jnp.where(core == 0, block[:count], block[16 - count :])

        for channel in range(3):
            rows[level, 2 * channel : 2 * channel + 2, :] = ends(stage[level // 2, channel, level % 2], 2)
        rows[level, 6:9, :] = ends(stage[level // 2, 3, level % 2], 3)
        rows[level, 9:10, :] = ends(stage_kd[level], 1)
    out_ref[...] = rows[...].astype(jnp.bfloat16)


def moved(kernel, scalars, inputs, outs, scratch, aliases=None, vmem_outs=0):
    smem = pl.BlockSpec(memory_space=pltpu.SMEM)
    anywhere = pl.BlockSpec(memory_space=pl.ANY)
    return pl.pallas_call(
        kernel,
        out_shape=tuple(jax.ShapeDtypeStruct(shape, jnp.bfloat16) for shape in outs),
        in_specs=[smem] * len(scalars) + [anywhere] * len(inputs),
        out_specs=(pl.BlockSpec(memory_space=pltpu.VMEM),) * vmem_outs + (anywhere,) * (len(outs) - vmem_outs),
        scratch_shapes=scratch,
        input_output_aliases=aliases or {},
        compiler_params=pltpu.CompilerParams(vmem_limit_bytes=12 * 2**20),
        cost_estimate=pl.CostEstimate(flops=0, bytes_accessed=2**21, transcendentals=0),
    )(*scalars, *inputs)


def exchange(sends):
    shifts = ((1, 0), (3, 0), (0, 1))
    arrived = []
    for send, (dz, dh) in zip(sends, shifts):
        pairs = []
        for z in range(4):
            for h in range(2):
                for core in range(2):
                    pairs.append((z * 4 + h * 2 + core, (z + dz) % 4 * 4 + (h ^ dh) * 2 + core))
        arrived.append(lax.ppermute(send, "rel", pairs))
    return arrived


def other_core(value):
    return lax.ppermute(value, "rel", [(i, i ^ 1) for i in range(16)])


def swap_ends(edges):
    ends = []
    for flip in range(2):
        pairs = []
        for slab in range(8):
            for rel in range(16):
                to = slab - 1 + 2 * (rel & 1)
                if 0 <= to < 8:
                    pairs.append((slab * 16 + rel, to * 16 + (rel ^ flip)))
        ends.append(lax.ppermute(edges, ("slab", "rel"), pairs))
    return ends


def broadcast(wind_store, ids, field):
    table = jnp.asarray(SCHEDULES, jnp.int32).reshape(-1)
    every = (2 * PIECES,) + PIECE
    dma = pltpu.SemaphoreType.DMA
    sent = [PIECE] * LINKS

    def stage(slots):
        return pltpu.VMEM((slots,) + PIECE, jnp.bfloat16)

    (shared,) = moved(share_kernel, (ids,), [wind_store], [every], [stage(2 * PIECES), dma((4 * PIECES,))])
    shared = other_core(shared)

    def begin(phase, keeps, wind_store, shared, arrived):
        return moved(
            functools.partial(first_kernel, phase, len(arrived), keeps), (ids, table), [wind_store, shared, *arrived],
            sent + [every] * keeps, [stage(2 * PIECES + LINKS), dma((4 * PIECES + LINKS,))],
        )

    def one_chip(wind_store, shared):
        return begin(1, True, wind_store, shared, exchange(begin(0, False, wind_store, shared, [])))

    *sends, held = lax.cond(
        ids[0] >> 2 == ids[1] >> 2, one_chip, lambda store, shared: begin(1, True, store, shared, []), wind_store, shared
    )
    ends = (field[:, :, :4], field[:, :, -4:])
    def keep(phase, arrived, held, lays):
        held, *older = moved(
            functools.partial(keep_kernel, phase, len(arrived), lays), (ids, table), [*arrived, held], [every] + sent * lays,
            [stage(2 * LINKS), dma((2 * LINKS,))], {2 + len(arrived): 0},
        )
        return held, older

    came = []
    for phase in range(1, PHASES + 1):
        if phase == 2:
            *ends, held = lax.optimization_barrier((*ends, held))
            west, east = halos(*ends)
        *sends, held = lax.optimization_barrier((*sends, held))
        held, older = keep(phase - 1, came, held, phase < PHASES)
        arrived = exchange(sends)
        if phase == 3:
            west, east, arrived[0] = lax.optimization_barrier((west, east, arrived[0]))
        if phase < PHASES:
            sends = moved(
                functools.partial(forward_kernel, phase), (ids, table), [*arrived, *older], sent, [stage(LINKS), dma((LINKS,))]
            )
            came = arrived
    (edges,) = moved(
        edge_kernel, (), [held], [(4, 16, 1024)],
        [stage(2), pltpu.VMEM((4, 16, 1024), jnp.bfloat16), pltpu.VMEM((4, 16, 1024), jnp.float32), dma((3,))],
        vmem_outs=1,
    )
    ends = swap_ends(edges)
    held, _ = keep(PHASES, arrived, held, False)
    *ends, held = lax.optimization_barrier((*ends, held))
    after, west, east, held = lax.optimization_barrier((field, west, east, held))
    return lay_out(after, west, east), held, other_core(held), *ends


def shifted_y(here, left, right, lane):
    south_one = pltpu.roll(jnp.where(lane == LANES - 1, left, here), 1, 1)
    south_two = pltpu.roll(jnp.where(lane >= LANES - 2, left, here), 2, 1)
    north_one = pltpu.roll(jnp.where(lane == 0, right, here), LANES - 1, 1)
    north_two = pltpu.roll(jnp.where(lane <= 1, right, here), LANES - 2, 1)
    return south_two, south_one, north_one, north_two


def upwind(courant):
    sixth = courant * (1.0 / 6.0)
    far = jnp.abs(sixth)
    near = far + far
    tilt = 4.0 * sixth
    return near + tilt, near - tilt, far


def roll_one(here, left, right, lane):
    south = pltpu.roll(jnp.where(lane == LANES - 1, left, here), 1, 1)
    north = pltpu.roll(jnp.where(lane == 0, right, here), LANES - 1, 1)
    return south, north


def weights(level, levels, cx, cy, cz, kd_here, kd_west, kd_east, kd_left, kd_right, lane):
    middle = kd_here[level]
    kd_south, kd_north = roll_one(middle, kd_left, kd_right, lane)
    west, east = middle + kd_west, middle + kd_east
    south, north = middle + kd_south, middle + kd_north
    below = middle + kd_here[max(level - 1, 0)]
    above = middle + kd_here[min(level + 1, levels - 1)]
    w1, e1, far_x = upwind(cx)
    s1, n1, far_y = upwind(cy)
    b1, a1, far_z = upwind(cz)
    loss = 3.0 * (far_x + far_y + far_z) + ((west + east) + (south + north) + (below + above))
    positive = jnp.maximum(cz * (1.0 / 6.0), 0.0)
    by_level = [None] * levels
    by_level[level] = 1.0 - loss
    for offset, weight in ((-2, -positive), (-1, b1 + below), (1, a1 + above), (2, positive - far_z)):
        at = min(max(level + offset, 0), levels - 1)
        by_level[at] = weight if by_level[at] is None else by_level[at] + weight
    return (cx > 0.0, far_x, w1 + west, e1 + east), (cy > 0.0, far_y, s1 + south, n1 + north), by_level


def weighted(along_x, along_y, by_level, level, x_cells, columns, left, right, lane):
    center = columns[level]
    y_cells = shifted_y(center, left, right, lane)
    total = by_level[level] * center
    for (forward, far, behind, ahead), cells in ((along_y, y_cells), (along_x, x_cells)):
        total = total + (behind * cells[1] + ahead * cells[2])
        total = total - far * jnp.where(forward, cells[0], cells[3])
    for other, weight in enumerate(by_level):
        if other != level and weight is not None:
            total = total + weight * columns[other]
    return total


def lay_out_kernel(field_hbm, west_ref, east_ref, out_ref, sems):
    chunks = out_ref.shape[2]
    rows = out_ref.shape[3] - 2 * PAD
    copies = []
    for j in range(chunks):
        span = pl.ds(j * LANES, LANES)
        copies.append((None, field_hbm.at[:, :, :, span], out_ref.at[:, :, j, pl.ds(PAD, rows), :], sems.at[j]))
        out_ref[:, :, j, PAD - 4 : PAD, :] = west_ref[:, :, :, span]
        out_ref[:, :, j, PAD + rows : PAD + rows + 4, :] = east_ref[:, :, :, span]
    run_copies(copies)


def lay_out(field, west, east):
    releases, levels, rows, width = field.shape
    chunks = width // LANES
    vmem = pl.BlockSpec(memory_space=pltpu.VMEM)
    return pl.pallas_call(
        lay_out_kernel,
        out_shape=jax.ShapeDtypeStruct((releases, levels, chunks, rows + 2 * PAD, LANES), jnp.float32),
        in_specs=[pl.BlockSpec(memory_space=pltpu.HBM), vmem, vmem],
        out_specs=vmem,
        scratch_shapes=[pltpu.SemaphoreType.DMA((chunks,))],
        compiler_params=pltpu.CompilerParams(vmem_limit_bytes=16 * 2**20),
        cost_estimate=pl.CostEstimate(flops=0, bytes_accessed=2**23, transcendentals=0),
    )(field, west, east)


def steps_kernel(cells_ref, amount_ref, first, mine_ref, other_ref, *rest):
    near_ref, far_ref, out_hbm, second, result, winds, half_kds, halo_wind, wind_sems, out_sems = rest
    releases, levels, chunks, padded_rows, _ = first.shape
    rows = padded_rows - 2 * PAD
    core = lax.rem(lax.axis_index("rel"), 2)
    slab = lax.axis_index("slab")

    def store(j):
        return pltpu.make_async_copy(
            result.at[:, :, j],
            out_hbm.at[:, :, :, pl.ds(pl.multiple_of(j * LANES, LANES), LANES)],
            out_sems.at[j],
        )

    wind_copies = []
    for slot in range(2 * PIECES):
        snap = slot // PIECES
        for number, (held, half) in enumerate(((mine_ref, core), (other_ref, 1 - core))):
            for part, (target, source) in enumerate(parts_of(snap, slot % PIECES, half, winds.at[snap], held.at[slot])):
                wind_copies.append((None, source, target, wind_sems.at[4 * slot + 2 * number + part]))
    run_copies(wind_copies, (True,))

    lane = lax.broadcasted_iota(jnp.int32, (8, LANES), 1)
    sublane = lax.broadcasted_iota(jnp.int32, (8, LANES), 0)
    lane_row = lax.broadcasted_iota(jnp.int32, (1, LANES), 1)

    def span_of(j):
        return pl.ds(pl.multiple_of(j * LANES, LANES), LANES)

    def halo_rows(j, carry):
        span = span_of(j)
        near = near_ref[:, :, span].astype(jnp.float32)
        far = far_ref[:, :, span].astype(jnp.float32)
        east = jnp.where(core == 0, near, far)
        west = jnp.where(core == 0, far, near)
        for channel in range(3):
            halo_wind[channel, :, j, 0:2, :] = east[:, 2 * channel : 2 * channel + 2]
            halo_wind[channel, :, j, 6:8, :] = west[:, 2 * channel : 2 * channel + 2]
        half_kds[0, :, j, PAD + rows : PAD + rows + 3, :] = 0.5 * east[:, 6:9]
        half_kds[0, :, j, PAD - 3 : PAD, :] = 0.5 * west[:, 6:9]
        half_kds[1, :, j, PAD + rows : PAD + rows + 1, :] = 0.5 * east[:, 9:10]
        half_kds[1, :, j, PAD - 1 : PAD, :] = 0.5 * west[:, 9:10]
        return carry

    lax.fori_loop(0, chunks, halo_rows, 0)
    run_copies(wind_copies, (False,))

    def spread_kd(j, carry):
        for snap in range(2):
            for level in range(levels):
                half_kds[snap, level, j, PAD : PAD + rows, :] = 0.5 * winds[snap, 3, level, :, span_of(j)].astype(jnp.float32)
        return carry

    lax.fori_loop(0, chunks, spread_kd, 0)

    def chunk(snap, source, target, pad, j):
        before = lax.rem(j + chunks - 1, chunks)
        after = lax.rem(j + 1, chunks)
        span = span_of(j)
        half_kd = half_kds.at[snap]

        for start in range(0, rows, 16):
            for level in range(levels):
                courant = [
                    winds[snap, channel, level, pl.ds(start, 16), span].astype(jnp.float32) for channel in range(3)
                ]
                for half in range(2):
                    at = PAD + start + 8 * half
                    here = pl.ds(at, 8)
                    cx, cy, cz = (value[8 * half : 8 * half + 8] for value in courant)
                    along_x, along_y, by_level = weights(
                        level, levels, cx, cy, cz,
                        [half_kd[other, j, here, :] for other in range(levels)],
                        half_kd[level, j, pl.ds(at - 1, 8), :], half_kd[level, j, pl.ds(at + 1, 8), :],
                        half_kd[level, before, here, :], half_kd[level, after, here, :], lane,
                    )
                    for release in range(releases):
                        target[release, level, j, pl.ds(at - PAD + pad, 8), :] = weighted(
                            along_x, along_y, by_level, level,
                            [source[release, level, j, pl.ds(at + shift, 8), :] for shift in (-2, -1, 1, 2)],
                            [source[release, other, j, here, :] for other in range(levels)],
                            source[release, level, before, here, :], source[release, level, after, here, :], lane,
                        )

    def halo_chunk(j):
        before = lax.rem(j + chunks - 1, chunks)
        after = lax.rem(j + 1, chunks)
        kept = jnp.logical_or(
            jnp.logical_and(sublane < 4, slab < lax.axis_size("slab") - 1), jnp.logical_and(sublane >= 4, slab > 0)
        )

        def around(ref, index, shift=0):
            east = ref[(*index, pl.ds(PAD + rows + shift, 8), slice(None))]
            west = ref[(*index, pl.ds(PAD - 8 + shift, 8), slice(None))]
            return jnp.where(sublane < 4, east, west)

        half_kd = half_kds.at[0]
        for level in range(levels):
            along_x, along_y, by_level = weights(
                level, levels, *(halo_wind[channel, level, j] for channel in range(3)),
                [around(half_kd, (other, j)) for other in range(levels)],
                around(half_kd, (level, j), -1), around(half_kd, (level, j), 1),
                around(half_kd, (level, before)), around(half_kd, (level, after)), lane,
            )
            for release in range(releases):
                value = weighted(
                    along_x, along_y, by_level, level,
                    [around(first, (release, level, j), shift) for shift in (-2, -1, 1, 2)],
                    [around(first, (release, other, j)) for other in range(levels)],
                    around(first, (release, level, before)), around(first, (release, level, after)), lane,
                )
                value = jnp.where(kept, value, 0.0)
                second[release, level, j, PAD + rows : PAD + rows + 4, :] = value[0:4]
                second[release, level, j, PAD - 4 : PAD, :] = value[4:8]

    def emit(ref, j, pad, reach):
        for release in range(releases):
            at_row = cells_ref[1, release]
            inside = jnp.logical_and(at_row >= -reach, at_row < rows + reach)
            amount = jnp.where(inside, amount_ref[release], 0.0)
            row = pad + jnp.clip(at_row, -reach, rows + reach - 1)
            spot = (release, cells_ref[0, release], j, pl.ds(row, 1), slice(None))
            ref[spot] = ref[spot] + jnp.where(j * LANES + lane_row == cells_ref[2, release], amount, 0.0)

    def first_step(j, carry):
        chunk(0, first, second, PAD, j)
        halo_chunk(j)
        emit(second, j, PAD, 2)
        return carry

    def second_step(j, carry):
        chunk(1, second, result, 0, j)
        emit(result, j, 0, 0)
        store(j).start()
        return carry

    lax.fori_loop(0, chunks, first_step, 0)
    lax.fori_loop(0, chunks, second_step, 0)
    for j in range(chunks):
        store(j).wait()


def steps(shape, start, mine, other, near, far, cells, amounts):
    releases, levels, rows, width = shape
    chunks = width // LANES
    vmem = pl.BlockSpec(memory_space=pltpu.VMEM)
    smem = pl.BlockSpec(memory_space=pltpu.SMEM)
    anywhere = pl.BlockSpec(memory_space=pl.ANY)
    return pl.pallas_call(
        steps_kernel,
        out_shape=jax.ShapeDtypeStruct(shape, jnp.float32),
        in_specs=[smem, smem, vmem, anywhere, anywhere, vmem, vmem],
        out_specs=pl.BlockSpec(memory_space=pltpu.HBM),
        scratch_shapes=[
            pltpu.VMEM(start.shape, jnp.float32),
            pltpu.VMEM((releases, levels, chunks, rows, LANES), jnp.float32),
            pltpu.VMEM((2, 4, levels, rows, width), jnp.bfloat16),
            pltpu.VMEM((2,) + start.shape[1:], jnp.float32),
            pltpu.VMEM((3, levels, chunks, 8, LANES), jnp.float32),
            pltpu.SemaphoreType.DMA((8 * PIECES,)),
            pltpu.SemaphoreType.DMA((chunks,)),
        ],
        compiler_params=pltpu.CompilerParams(vmem_limit_bytes=36 * 2**20),
        cost_estimate=pl.CostEstimate(flops=120 * math.prod(shape), bytes_accessed=12 * math.prod(shape), transcendentals=0),
    )(cells, amounts, start, mine, other, near, far)


def halos(first, last):
    count = lax.axis_size("slab")
    up = [(i, (i + 1) % count) for i in range(count - 1)]
    down = [(j, i) for i, j in up]
    return lax.ppermute(last, "slab", up), lax.ppermute(first, "slab", down)


def body(concentration, wind_store, sources, emission, snapshot_ids):
    rows, width = concentration.shape[2:]
    full = rows * lax.axis_size("slab")
    cells = jnp.stack([
        sources // (full * width),
        sources // width % full - lax.axis_index("slab") * rows,
        sources % width,
    ])
    return steps(concentration.shape, *broadcast(wind_store, snapshot_ids, concentration), cells, emission)


def solution(mesh):
    placed = (
        P("rel", None, "slab", None),
        P("rel", None, None, "slab", None),
        P("rel"),
        P("rel"),
        P(),
    )
    return jax.shard_map(
        body, mesh=mesh, in_specs=placed, out_specs=P("rel", None, "slab", None), check_vma=False
    )
```

```python
import functools
import math
import jax
import jax.numpy as jnp
from jax import lax
from jax.experimental import pallas as pl
from jax.experimental.pallas import tpu as pltpu
from jax.sharding import PartitionSpec as P

LANES = 128
PAD = 16


PIECES = 4
PIECE = (4, 2, 16, 1024)
LINKS = 3
PHASES = 4

SCHEDULES = (
    (
        (4, 5, 0, -1, -1, -1, -1, -1, -1, -1, -1, -1, -1, -1, -1, -1, -1, -1, -1, -1, -1, -1, -1, -1),
        (3, 1, 7, -1, 0, -1, 4, -1, 4, -1, -1, -1, -1, -1, -1, -1, -1, -1, -1, 5, 5, -1, -1, -1),
        (1, 2, 6, 7, -1, -1, -1, -1, 3, -1, -1, -1, -1, 5, 4, -1, -1, -1, -1, 1, 1, 5, 0, 0),
        (0, 6, 2, 6, 7, -1, 3, -1, 1, 3, 4, 7, 4, 4, 1, 4, 0, 0, -1, 2, 2, 1, 5, -1),
        (5, 7, 3, 2, -1, -1, 7, -1, 3, 6, 7, 6, 3, 2, 2, 3, 5, -1, -1, 6, 6, -1, 7, 2),
    ),
    (
        (-1, -1, -1, -1, -1, -1, -1, -1, -1, -1, -1, -1, -1, -1, -1, -1, -1, -1, -1, -1, -1, -1, -1, -1),
        (1, 3, 0, 6, 4, 4, -1, -1, -1, -1, -1, -1, -1, -1, -1, -1, -1, -1, -1, -1, -1, -1, -1, -1),
        (0, 2, 1, 5, 0, 7, 1, -1, 1, 6, -1, -1, -1, -1, -1, -1, -1, -1, -1, 3, 3, -1, 4, 4),
        (4, 7, 2, 7, 1, 5, 0, -1, 0, 5, -1, 5, 1, 3, 1, 6, 4, 4, -1, 2, 4, -1, 0, 0),
        (7, 5, 3, 2, 7, 6, 5, -1, 3, 7, -1, 6, 3, 2, 2, 5, 5, 6, -1, 7, 2, -1, 3, 6),
    ),
    (
        (-1, -1, -1, -1, -1, -1, -1, -1, -1, -1, -1, -1, -1, -1, -1, -1, -1, -1, -1, -1, -1, -1, -1, -1),
        (1, 0, 1, -1, -1, -1, 6, 5, 4, -1, -1, -1, -1, -1, -1, -1, -1, -1, -1, -1, -1, -1, -1, -1),
        (0, 3, 2, 1, 1, -1, 5, 4, 7, 4, 4, -1, 6, -1, 6, -1, -1, -1, -1, 0, 0, -1, -1, -1),
        (2, 4, 3, 2, 2, -1, 1, 7, 0, 7, 7, -1, 5, -1, 0, 4, 6, 4, -1, 3, 3, 0, 1, 1),
        (2, 7, 5, 3, 7, -1, 2, 7, 5, 2, 6, -1, 5, 3, 5, 6, -1, 7, 6, -1, 5, -1, 3, 2),
    ),
    (
        (-1, -1, -1, -1, -1, -1, -1, -1, -1, -1, -1, -1, -1, -1, -1, -1, -1, -1, -1, -1, -1, -1, -1, -1),
        (0, 1, 0, -1, -1, -1, -1, -1, -1, 4, 5, 6, -1, -1, -1, -1, -1, -1, -1, -1, -1, -1, -1, -1),
        (1, 2, 3, -1, 0, 5, 0, -1, 0, 7, 6, 4, -1, -1, -1, 4, -1, 4, -1, 1, 1, -1, -1, -1),
        (3, 5, 2, 3, 6, -1, 6, 4, 1, 5, 4, 7, 0, 1, 1, -1, -1, 7, 1, 2, 2, 1, 0, 4),
        (5, 3, 5, 2, 3, 6, 3, 7, 6, 3, 7, 7, 7, 2, 2, 7, -1, 7, -1, 5, 5, 2, 6, 6),
    ),
    (
        (-1, -1, -1, -1, -1, -1, -1, -1, -1, -1, -1, -1, -1, -1, -1, -1, -1, -1, -1, -1, -1, -1, -1, -1),
        (0, 0, 1, -1, -1, -1, -1, -1, -1, -1, -1, -1, 4, 6, 4, -1, -1, -1, -1, -1, -1, -1, -1, -1),
        (3, 1, 2, 1, 1, -1, -1, 6, 0, -1, -1, -1, 6, 7, 5, 4, 4, -1, -1, -1, 0, -1, -1, -1),
        (3, 2, 3, 2, 2, -1, 0, 7, 3, 1, 4, 1, 5, 4, 7, 5, 5, 5, 4, 1, 6, 0, 0, -1),
        (7, 3, 7, 3, 3, -1, 3, 6, 6, 3, 5, 2, 7, 5, 6, 7, 7, -1, 5, 2, 2, 6, 2, 6),
    ),
    (
        (-1, -1, -1, -1, -1, -1, -1, -1, -1, -1, -1, -1, -1, -1, -1, -1, -1, -1, -1, -1, -1, -1, -1, -1),
        (1, 2, 0, -1, -1, -1, -1, -1, -1, -1, -1, -1, -1, -1, -1, 6, 4, 7, -1, -1, -1, -1, -1, -1),
        (0, 3, 1, 0, 0, -1, 1, -1, 1, -1, 4, -1, -1, 7, -1, 5, 6, 4, 2, -1, 2, 6, -1, 6),
        (2, 1, 3, -1, 1, 4, 0, 7, -1, 1, 0, 6, 4, 4, 7, 4, 5, -1, -1, 3, 6, 5, 0, 0),
        (7, 7, 7, 3, 3, 5, 2, 2, 2, -1, -1, 5, 3, 3, 3, 7, 7, 5, 6, 6, 2, 2, 2, 5),
    ),
    (
        (-1, -1, -1, -1, -1, -1, -1, -1, -1, -1, -1, -1, -1, -1, -1, -1, -1, -1, -1, -1, -1, -1, -1, -1),
        (0, 0, 1, -1, -1, -1, -1, -1, -1, -1, -1, -1, -1, -1, -1, -1, -1, -1, 6, 7, 4, -1, -1, -1),
        (3, 1, 2, 1, 1, -1, 0, -1, 0, -1, -1, -1, -1, 7, 7, -1, -1, -1, 4, 5, 6, 4, 4, -1),
        (4, 2, 3, 2, 2, -1, -1, 7, 3, 1, 0, 1, -1, 5, 0, 7, 4, 4, 5, 1, 0, 6, 6, -1),
        (6, 3, 5, 6, 3, -1, 3, -1, 5, 3, -1, 2, -1, -1, 5, -1, 7, 6, -1, 2, 5, 7, 2, -1),
    ),
    (
        (-1, -1, -1, -1, -1, -1, -1, -1, -1, -1, -1, -1, -1, -1, -1, -1, -1, -1, -1, -1, -1, -1, -1, -1),
        (0, 1, 2, -1, -1, -1, -1, -1, -1, -1, -1, -1, -1, -1, -1, -1, -1, -1, -1, -1, -1, 4, 7, 4),
        (1, 3, 0, 4, -1, -1, 0, -1, 0, -1, -1, -1, -1, -1, -1, -1, 7, -1, -1, 4, 1, 5, 6, 5),
        (3, 2, 1, 2, 0, 5, 1, -1, 1, 4, 0, 7, 0, 4, 0, -1, 6, 7, 4, 5, 3, 5, 1, 6),
        (2, 2, 3, 5, 2, -1, 3, 7, 3, 2, 6, 6, 7, 5, 5, 7, -1, 6, 6, 2, 6, 7, 3, 5),
    ),
)


def parts_of(snap, piece, half, tile, held):
    if snap == 0:
        at = pl.multiple_of(half * 32 + 16 * ((piece // 2) ^ half), 16)
        return [(tile.at[:, pl.ds(2 * (piece % 2), 2), pl.ds(at, 16), :], held)]
    return [
        (tile.at[(piece + 3) % 4, :, pl.ds(pl.multiple_of(half * 32 + 16 * part, 16), 16), :], held.at[:, part])
        for part in range(2)
    ]


def plan(ids_ref, table_ref):
    chip = lax.axis_index("rel") >> 1
    first = ids_ref[0] >> 2
    second = ids_ref[1] >> 2

    def place(of):
        return 2 * (((of >> 1) - (first >> 1)) & 3) + ((of ^ first) & 1)

    here = place(chip)
    row = place(second) * 5
    z, h = here >> 1, here & 1
    sources = (2 * ((z - 1) & 3) + h, 2 * ((z + 1) & 3) + h, 2 * z + 1 - h)

    def sent(phase, link):
        return table_ref[(row + phase) * 24 + here * LINKS + link]

    def got(phase, link):
        return table_ref[(row + phase) * 24 + sources[link] * LINKS + link]

    return sent, got


def run_copies(copies, stages=(True, False)):
    for begin in stages:
        for condition, source, target, sem in copies:
            def act(source=source, target=target, sem=sem):
                copy = pltpu.make_async_copy(source, target, sem)
                if begin:
                    copy.start()
                else:
                    copy.wait()
            if condition is None:
                act()
            else:
                pl.when(condition)(act)


def run_staged(loads, stores):
    run_copies(loads)
    run_copies(stores)


def share_kernel(ids_ref, store_ref, out_ref, stage, sems):
    core = lax.axis_index("rel") & 1
    slots = range(2 * PIECES)
    loads = []
    for slot in slots:
        store = store_ref.at[ids_ref[slot // PIECES] & 1]
        for part, (source, target) in enumerate(parts_of(slot // PIECES, slot % PIECES, 1 - core, store, stage.at[slot])):
            loads.append((None, source, target, sems.at[2 * slot + part]))
    run_staged(loads, [(None, stage.at[slot], out_ref.at[slot], sems.at[slot]) for slot in slots])


def first_kernel(phase, brought, keeps, ids_ref, table_ref, store_ref, shared_ref, *rest):
    arrived, outs, held_ref = rest[:brought], rest[brought : brought + LINKS], rest[brought + LINKS]
    stage, sems = rest[-2:]
    me = lax.axis_index("rel")
    core = me & 1
    sent, got = plan(ids_ref, table_ref)
    loads, stores = [], []
    for slot in range(2 * PIECES):
        root = ids_ref[slot // PIECES] >> 1
        store = store_ref.at[ids_ref[slot // PIECES] & 1]
        for part, (source, target) in enumerate(parts_of(slot // PIECES, slot % PIECES, core, store, stage.at[slot])):
            loads.append((root == me, source, target, sems.at[2 * slot + part]))
        loads.append((root == (me ^ 1), shared_ref.at[slot], stage.at[slot], sems.at[2 * slot]))
        held = (root >> 1) == (me >> 1)
        for link in range(LINKS):
            chosen = jnp.logical_and(held, sent(phase, link) == slot)
            stores.append((chosen, stage.at[slot], outs[link], sems.at[link]))
        if keeps:
            stores.append((held, stage.at[slot], held_ref.at[slot], sems.at[2 * LINKS + slot]))
    for way in range(brought):
        slot = got(0, way)
        at = 2 * PIECES + way
        loads.append((None, arrived[way], stage.at[at], sems.at[4 * PIECES + way]))
        for link in range(LINKS):
            chosen = jnp.logical_and(slot >= 0, sent(phase, link) == slot)
            stores.append((chosen, stage.at[at], outs[link], sems.at[link]))
        stores.append((slot >= 0, stage.at[at], held_ref.at[jnp.maximum(slot, 0)], sems.at[LINKS + way]))
    run_staged(loads, stores)


def forward_kernel(phase, ids_ref, table_ref, *rest):
    arrived, older, outs, stage, sems = rest[:LINKS], rest[LINKS : 2 * LINKS], rest[2 * LINKS : -2], rest[-2], rest[-1]
    sent, got = plan(ids_ref, table_ref)
    loads, stores = [], []
    for link in range(LINKS):
        slot = sent(phase + 1, link)
        loads.extend(
            (condition, source, stage.at[link], sems.at[link])
            for condition, source in wherever(slot, phase, got, arrived, older[link])
        )
        stores.append((slot >= 0, stage.at[link], outs[link], sems.at[link]))
    run_staged(loads, stores)


def keep_kernel(phase, brought, lays, ids_ref, table_ref, *rest):
    arrived, held_in, held_ref, outs = rest[:brought], rest[brought], rest[brought + 1], rest[brought + 2 : -2]
    stage, sems = rest[-2:]
    sent, got = plan(ids_ref, table_ref)
    loads, stores = [], []
    for way in range(brought):
        slot = got(phase, way)
        loads.append((slot >= 0, arrived[way], stage.at[way], sems.at[way]))
        stores.append((slot >= 0, stage.at[way], held_ref.at[jnp.maximum(slot, 0)], sems.at[way]))
    for link in range(LINKS * lays):
        slot = sent(phase + 2, link)
        at = LINKS + link
        older = slot >= 0
        for way in range(LINKS):
            older = jnp.logical_and(older, got(phase + 1, way) != slot)
        before = older
        for way in range(brought):
            now = got(phase, way) == slot
            stores.append((jnp.logical_and(older, now), stage.at[way], outs[link], sems.at[at]))
            before = jnp.logical_and(before, jnp.logical_not(now))
        loads.append((before, held_in.at[jnp.maximum(slot, 0)], stage.at[at], sems.at[at]))
        stores.append((before, stage.at[at], outs[link], sems.at[at]))
    run_staged(loads, stores)


def wherever(slot, phase, got, arrived, older_ref):
    older = slot >= 0
    places = []
    for way in range(LINKS):
        places.append((jnp.logical_and(slot >= 0, got(phase, way) == slot), arrived[way]))
        older = jnp.logical_and(older, got(phase, way) != slot)
    return [*places, (older, older_ref)]


def edge_kernel(held_ref, out_ref, stage, stage_kd, rows, sems):
    core = lax.axis_index("rel") & 1
    run_copies([
        (None, held_ref.at[0], stage.at[0], sems.at[0]),
        (None, held_ref.at[1], stage.at[1], sems.at[1]),
        (None, held_ref.at[PIECES, :, core], stage_kd, sems.at[2]),
    ])
    rows[:, 10:, :] = jnp.zeros_like(rows[:, 10:, :])
    for level in range(4):
        def ends(block, count):
            block = block.astype(jnp.float32)
            return jnp.where(core == 0, block[:count], block[16 - count :])

        for channel in range(3):
            rows[level, 2 * channel : 2 * channel + 2, :] = ends(stage[level // 2, channel, level % 2], 2)
        rows[level, 6:9, :] = ends(stage[level // 2, 3, level % 2], 3)
        rows[level, 9:10, :] = ends(stage_kd[level], 1)
    out_ref[...] = rows[...].astype(jnp.bfloat16)


def moved(kernel, scalars, inputs, outs, scratch, aliases=None, vmem_outs=0):
    smem = pl.BlockSpec(memory_space=pltpu.SMEM)
    anywhere = pl.BlockSpec(memory_space=pl.ANY)
    return pl.pallas_call(
        kernel,
        out_shape=tuple(jax.ShapeDtypeStruct(shape, jnp.bfloat16) for shape in outs),
        in_specs=[smem] * len(scalars) + [anywhere] * len(inputs),
        out_specs=(pl.BlockSpec(memory_space=pltpu.VMEM),) * vmem_outs + (anywhere,) * (len(outs) - vmem_outs),
        scratch_shapes=scratch,
        input_output_aliases=aliases or {},
        compiler_params=pltpu.CompilerParams(vmem_limit_bytes=12 * 2**20),
        cost_estimate=pl.CostEstimate(flops=0, bytes_accessed=2**21, transcendentals=0),
    )(*scalars, *inputs)


def exchange(sends):
    shifts = ((1, 0), (3, 0), (0, 1))
    arrived = []
    for send, (dz, dh) in zip(sends, shifts):
        pairs = []
        for z in range(4):
            for h in range(2):
                for core in range(2):
                    pairs.append((z * 4 + h * 2 + core, (z + dz) % 4 * 4 + (h ^ dh) * 2 + core))
        arrived.append(lax.ppermute(send, "rel", pairs))
    return arrived


def other_core(value):
    return lax.ppermute(value, "rel", [(i, i ^ 1) for i in range(16)])


def swap_ends(edges):
    ends = []
    for flip in range(2):
        pairs = []
        for slab in range(8):
            for rel in range(16):
                to = slab - 1 + 2 * (rel & 1)
                if 0 <= to < 8:
                    pairs.append((slab * 16 + rel, to * 16 + (rel ^ flip)))
        ends.append(lax.ppermute(edges, ("slab", "rel"), pairs))
    return ends


def broadcast(wind_store, ids, field):
    table = jnp.asarray(SCHEDULES, jnp.int32).reshape(-1)
    every = (2 * PIECES,) + PIECE
    dma = pltpu.SemaphoreType.DMA
    sent = [PIECE] * LINKS

    def stage(slots):
        return pltpu.VMEM((slots,) + PIECE, jnp.bfloat16)

    (shared,) = moved(share_kernel, (ids,), [wind_store], [every], [stage(2 * PIECES), dma((4 * PIECES,))])
    shared = other_core(shared)

    def begin(phase, keeps, wind_store, shared, arrived):
        return moved(
            functools.partial(first_kernel, phase, len(arrived), keeps), (ids, table), [wind_store, shared, *arrived],
            sent + [every] * keeps, [stage(2 * PIECES + LINKS), dma((4 * PIECES + LINKS,))],
        )

    def one_chip(wind_store, shared):
        return begin(1, True, wind_store, shared, exchange(begin(0, False, wind_store, shared, [])))

    *sends, held = lax.cond(
        ids[0] >> 2 == ids[1] >> 2, one_chip, lambda store, shared: begin(1, True, store, shared, []), wind_store, shared
    )
    ends = (field[:, :, :4], field[:, :, -4:])
    def keep(phase, arrived, held, lays):
        held, *older = moved(
            functools.partial(keep_kernel, phase, len(arrived), lays), (ids, table), [*arrived, held], [every] + sent * lays,
            [stage(2 * LINKS), dma((2 * LINKS,))], {2 + len(arrived): 0},
        )
        return held, older

    came = []
    for phase in range(1, PHASES + 1):
        if phase == 2:
            *ends, held = lax.optimization_barrier((*ends, held))
            west, east = halos(*ends)
        *sends, held = lax.optimization_barrier((*sends, held))
        held, older = keep(phase - 1, came, held, phase < PHASES)
        arrived = exchange(sends)
        if phase == 3:
            west, east, arrived[0] = lax.optimization_barrier((west, east, arrived[0]))
        if phase < PHASES:
            sends = moved(
                functools.partial(forward_kernel, phase), (ids, table), [*arrived, *older], sent, [stage(LINKS), dma((LINKS,))]
            )
            came = arrived
    (edges,) = moved(
        edge_kernel, (), [held], [(4, 16, 1024)],
        [stage(2), pltpu.VMEM((4, 16, 1024), jnp.bfloat16), pltpu.VMEM((4, 16, 1024), jnp.float32), dma((3,))],
        vmem_outs=1,
    )
    ends = swap_ends(edges)
    held, _ = keep(PHASES, arrived, held, False)
    *ends, held = lax.optimization_barrier((*ends, held))
    after, west, east, held = lax.optimization_barrier((field, west, east, held))
    return lay_out(after, west, east), held, other_core(held), *ends


def shifted_y(here, left, right, lane):
    south_one = pltpu.roll(jnp.where(lane == LANES - 1, left, here), 1, 1)
    south_two = pltpu.roll(jnp.where(lane >= LANES - 2, left, here), 2, 1)
    north_one = pltpu.roll(jnp.where(lane == 0, right, here), LANES - 1, 1)
    north_two = pltpu.roll(jnp.where(lane <= 1, right, here), LANES - 2, 1)
    return south_two, south_one, north_one, north_two


def upwind(courant):
    sixth = courant * (1.0 / 6.0)
    far = jnp.abs(sixth)
    near = far + far
    tilt = 4.0 * sixth
    return near + tilt, near - tilt, far


def roll_one(here, left, right, lane):
    south = pltpu.roll(jnp.where(lane == LANES - 1, left, here), 1, 1)
    north = pltpu.roll(jnp.where(lane == 0, right, here), LANES - 1, 1)
    return south, north


def weights(level, levels, cx, cy, cz, kd_here, kd_west, kd_east, kd_left, kd_right, lane):
    middle = kd_here[level]
    kd_south, kd_north = roll_one(middle, kd_left, kd_right, lane)
    west, east = middle + kd_west, middle + kd_east
    south, north = middle + kd_south, middle + kd_north
    below = middle + kd_here[max(level - 1, 0)]
    above = middle + kd_here[min(level + 1, levels - 1)]
    w1, e1, far_x = upwind(cx)
    s1, n1, far_y = upwind(cy)
    b1, a1, far_z = upwind(cz)
    loss = 3.0 * (far_x + far_y + far_z) + ((west + east) + (south + north) + (below + above))
    positive = jnp.maximum(cz * (1.0 / 6.0), 0.0)
    by_level = [None] * levels
    by_level[level] = 1.0 - loss
    for offset, weight in ((-2, -positive), (-1, b1 + below), (1, a1 + above), (2, positive - far_z)):
        at = min(max(level + offset, 0), levels - 1)
        by_level[at] = weight if by_level[at] is None else by_level[at] + weight
    return (cx > 0.0, far_x, w1 + west, e1 + east), (cy > 0.0, far_y, s1 + south, n1 + north), by_level


def weighted(along_x, along_y, by_level, level, x_cells, columns, left, right, lane):
    center = columns[level]
    y_cells = shifted_y(center, left, right, lane)
    total = by_level[level] * center
    for (forward, far, behind, ahead), cells in ((along_y, y_cells), (along_x, x_cells)):
        total = total + (behind * cells[1] + ahead * cells[2])
        total = total - far * jnp.where(forward, cells[0], cells[3])
    for other, weight in enumerate(by_level):
        if other != level and weight is not None:
            total = total + weight * columns[other]
    return total


def lay_out_kernel(field_hbm, west_ref, east_ref, out_ref, sems):
    chunks = out_ref.shape[2]
    rows = out_ref.shape[3] - 2 * PAD
    copies = []
    for j in range(chunks):
        span = pl.ds(j * LANES, LANES)
        copies.append((None, field_hbm.at[:, :, :, span], out_ref.at[:, :, j, pl.ds(PAD, rows), :], sems.at[j]))
        out_ref[:, :, j, PAD - 4 : PAD, :] = west_ref[:, :, :, span]
        out_ref[:, :, j, PAD + rows : PAD + rows + 4, :] = east_ref[:, :, :, span]
    run_copies(copies)


def lay_out(field, west, east):
    releases, levels, rows, width = field.shape
    chunks = width // LANES
    vmem = pl.BlockSpec(memory_space=pltpu.VMEM)
    return pl.pallas_call(
        lay_out_kernel,
        out_shape=jax.ShapeDtypeStruct((releases, levels, chunks, rows + 2 * PAD, LANES), jnp.float32),
        in_specs=[pl.BlockSpec(memory_space=pltpu.HBM), vmem, vmem],
        out_specs=vmem,
        scratch_shapes=[pltpu.SemaphoreType.DMA((chunks,))],
        compiler_params=pltpu.CompilerParams(vmem_limit_bytes=16 * 2**20),
        cost_estimate=pl.CostEstimate(flops=0, bytes_accessed=2**23, transcendentals=0),
    )(field, west, east)


def steps_kernel(cells_ref, amount_ref, first, mine_ref, other_ref, *rest):
    near_ref, far_ref, out_hbm, second, result, winds, half_kds, halo_wind, wind_sems, out_sems = rest
    releases, levels, chunks, padded_rows, _ = first.shape
    rows = padded_rows - 2 * PAD
    core = lax.rem(lax.axis_index("rel"), 2)
    slab = lax.axis_index("slab")

    def store(j):
        return pltpu.make_async_copy(
            result.at[:, :, j],
            out_hbm.at[:, :, :, pl.ds(pl.multiple_of(j * LANES, LANES), LANES)],
            out_sems.at[j],
        )

    wind_copies = []
    for slot in range(2 * PIECES):
        snap = slot // PIECES
        for number, (held, half) in enumerate(((mine_ref, core), (other_ref, 1 - core))):
            for part, (target, source) in enumerate(parts_of(snap, slot % PIECES, half, winds.at[snap], held.at[slot])):
                wind_copies.append((None, source, target, wind_sems.at[4 * slot + 2 * number + part]))
    run_copies(wind_copies, (True,))

    lane = lax.broadcasted_iota(jnp.int32, (8, LANES), 1)
    sublane = lax.broadcasted_iota(jnp.int32, (8, LANES), 0)
    lane_row = lax.broadcasted_iota(jnp.int32, (1, LANES), 1)

    def span_of(j):
        return pl.ds(pl.multiple_of(j * LANES, LANES), LANES)

    def halo_rows(j, carry):
        span = span_of(j)
        near = near_ref[:, :, span].astype(jnp.float32)
        far = far_ref[:, :, span].astype(jnp.float32)
        east = jnp.where(core == 0, near, far)
        west = jnp.where(core == 0, far, near)
        for channel in range(3):
            halo_wind[channel, :, j, 0:2, :] = east[:, 2 * channel : 2 * channel + 2]
            halo_wind[channel, :, j, 6:8, :] = west[:, 2 * channel : 2 * channel + 2]
        half_kds[0, :, j, PAD + rows : PAD + rows + 3, :] = 0.5 * east[:, 6:9]
        half_kds[0, :, j, PAD - 3 : PAD, :] = 0.5 * west[:, 6:9]
        half_kds[1, :, j, PAD + rows : PAD + rows + 1, :] = 0.5 * east[:, 9:10]
        half_kds[1, :, j, PAD - 1 : PAD, :] = 0.5 * west[:, 9:10]
        return carry

    lax.fori_loop(0, chunks, halo_rows, 0)
    run_copies(wind_copies[: 2 * PIECES], (False,))

    def spread_kd(snap, j, carry):
        for level in range(levels):
            half_kds[snap, level, j, PAD : PAD + rows, :] = 0.5 * winds[snap, 3, level, :, span_of(j)].astype(jnp.float32)
        return carry

    lax.fori_loop(0, chunks, functools.partial(spread_kd, 0), 0)

    def chunk(snap, source, target, pad, j):
        before = lax.rem(j + chunks - 1, chunks)
        after = lax.rem(j + 1, chunks)
        span = span_of(j)
        half_kd = half_kds.at[snap]

        for start in range(0, rows, 16):
            for level in range(levels):
                courant = [
                    winds[snap, channel, level, pl.ds(start, 16), span].astype(jnp.float32) for channel in range(3)
                ]
                for half in range(2):
                    at = PAD + start + 8 * half
                    here = pl.ds(at, 8)
                    cx, cy, cz = (value[8 * half : 8 * half + 8] for value in courant)
                    along_x, along_y, by_level = weights(
                        level, levels, cx, cy, cz,
                        [half_kd[other, j, here, :] for other in range(levels)],
                        half_kd[level, j, pl.ds(at - 1, 8), :], half_kd[level, j, pl.ds(at + 1, 8), :],
                        half_kd[level, before, here, :], half_kd[level, after, here, :], lane,
                    )
                    for release in range(releases):
                        target[release, level, j, pl.ds(at - PAD + pad, 8), :] = weighted(
                            along_x, along_y, by_level, level,
                            [source[release, level, j, pl.ds(at + shift, 8), :] for shift in (-2, -1, 1, 2)],
                            [source[release, other, j, here, :] for other in range(levels)],
                            source[release, level, before, here, :], source[release, level, after, here, :], lane,
                        )

    def halo_chunk(j):
        before = lax.rem(j + chunks - 1, chunks)
        after = lax.rem(j + 1, chunks)
        kept = jnp.logical_or(
            jnp.logical_and(sublane < 4, slab < lax.axis_size("slab") - 1), jnp.logical_and(sublane >= 4, slab > 0)
        )

        def around(ref, index, shift=0):
            east = ref[(*index, pl.ds(PAD + rows + shift, 8), slice(None))]
            west = ref[(*index, pl.ds(PAD - 8 + shift, 8), slice(None))]
            return jnp.where(sublane < 4, east, west)

        half_kd = half_kds.at[0]
        for level in range(levels):
            along_x, along_y, by_level = weights(
                level, levels, *(halo_wind[channel, level, j] for channel in range(3)),
                [around(half_kd, (other, j)) for other in range(levels)],
                around(half_kd, (level, j), -1), around(half_kd, (level, j), 1),
                around(half_kd, (level, before)), around(half_kd, (level, after)), lane,
            )
            for release in range(releases):
                value = weighted(
                    along_x, along_y, by_level, level,
                    [around(first, (release, level, j), shift) for shift in (-2, -1, 1, 2)],
                    [around(first, (release, other, j)) for other in range(levels)],
                    around(first, (release, level, before)), around(first, (release, level, after)), lane,
                )
                value = jnp.where(kept, value, 0.0)
                second[release, level, j, PAD + rows : PAD + rows + 4, :] = value[0:4]
                second[release, level, j, PAD - 4 : PAD, :] = value[4:8]

    def emit(ref, j, pad, reach):
        for release in range(releases):
            at_row = cells_ref[1, release]
            inside = jnp.logical_and(at_row >= -reach, at_row < rows + reach)
            amount = jnp.where(inside, amount_ref[release], 0.0)
            row = pad + jnp.clip(at_row, -reach, rows + reach - 1)
            spot = (release, cells_ref[0, release], j, pl.ds(row, 1), slice(None))
            ref[spot] = ref[spot] + jnp.where(j * LANES + lane_row == cells_ref[2, release], amount, 0.0)

    def first_step(j, carry):
        chunk(0, first, second, PAD, j)
        halo_chunk(j)
        emit(second, j, PAD, 2)
        return carry

    def second_step(j, carry):
        chunk(1, second, result, 0, j)
        emit(result, j, 0, 0)
        store(j).start()
        return carry

    lax.fori_loop(0, chunks, first_step, 0)
    run_copies(wind_copies[2 * PIECES :], (False,))
    lax.fori_loop(0, chunks, functools.partial(spread_kd, 1), 0)
    lax.fori_loop(0, chunks, second_step, 0)
    for j in range(chunks):
        store(j).wait()


def steps(shape, start, mine, other, near, far, cells, amounts):
    releases, levels, rows, width = shape
    chunks = width // LANES
    vmem = pl.BlockSpec(memory_space=pltpu.VMEM)
    smem = pl.BlockSpec(memory_space=pltpu.SMEM)
    anywhere = pl.BlockSpec(memory_space=pl.ANY)
    return pl.pallas_call(
        steps_kernel,
        out_shape=jax.ShapeDtypeStruct(shape, jnp.float32),
        in_specs=[smem, smem, vmem, anywhere, anywhere, vmem, vmem],
        out_specs=pl.BlockSpec(memory_space=pltpu.HBM),
        scratch_shapes=[
            pltpu.VMEM(start.shape, jnp.float32),
            pltpu.VMEM((releases, levels, chunks, rows, LANES), jnp.float32),
            pltpu.VMEM((2, 4, levels, rows, width), jnp.bfloat16),
            pltpu.VMEM((2,) + start.shape[1:], jnp.float32),
            pltpu.VMEM((3, levels, chunks, 8, LANES), jnp.float32),
            pltpu.SemaphoreType.DMA((8 * PIECES,)),
            pltpu.SemaphoreType.DMA((chunks,)),
        ],
        compiler_params=pltpu.CompilerParams(vmem_limit_bytes=36 * 2**20),
        cost_estimate=pl.CostEstimate(flops=120 * math.prod(shape), bytes_accessed=12 * math.prod(shape), transcendentals=0),
    )(cells, amounts, start, mine, other, near, far)


def halos(first, last):
    count = lax.axis_size("slab")
    up = [(i, (i + 1) % count) for i in range(count - 1)]
    down = [(j, i) for i, j in up]
    return lax.ppermute(last, "slab", up), lax.ppermute(first, "slab", down)


def body(concentration, wind_store, sources, emission, snapshot_ids):
    rows, width = concentration.shape[2:]
    full = rows * lax.axis_size("slab")
    cells = jnp.stack([
        sources // (full * width),
        sources // width % full - lax.axis_index("slab") * rows,
        sources % width,
    ])
    return steps(concentration.shape, *broadcast(wind_store, snapshot_ids, concentration), cells, emission)


def solution(mesh):
    placed = (
        P("rel", None, "slab", None),
        P("rel", None, None, "slab", None),
        P("rel"),
        P("rel"),
        P(),
    )
    return jax.shard_map(
        body, mesh=mesh, in_specs=placed, out_specs=P("rel", None, "slab", None), check_vma=False
    )
```
